512 devices in a mesh: gx: 32 (over z, core), gy: 16 (over y, x).
Axes of the slice: x: 4, y: 4, z: 16, core: 2. Of those that a mesh axis runs over, the one named last changes fastest.
Arguments:
- solution: float32 [512, 65536], P(None, ('gx', 'gy')), may hold values from -6 to 6
- residual: float32 [512, 65536], P(None, ('gx', 'gy')), may hold values from -60 to 60
- metric_diag: bfloat16 [3, 512, 65536], P(None, None, ('gx', 'gy')), may hold values from 0.039794922 to 0.3984375
- metric_cross: bfloat16 [3, 512, 65536], P(None, None, ('gx', 'gy')), may hold values from -0.017944336 to 0.017944336
- fdm_vectors: float32 [3, 8, 8, 65536], P(None, None, None, ('gx', 'gy')), may hold values from -5 to 5
- fdm_values: float32 [3, 8, 65536], P(None, None, ('gx', 'gy')), may hold values from 0.05 to 20
- vertex_ids: int32 [8, 65536], P(None, ('gx', 'gy')), may hold values from 0 to 8191
- coarse_inverse: float32 [8192, 8192], P(('gx', 'gy')), may hold values from -0.2 to 0.2, as said below
- elem_live: int32 [512], P(('gx', 'gy')), may hold values from 80 to 128, as said below
- section_face: int32 [512, 16, 20], P(('gx', 'gy')), may hold values from -1 to 767, as said below
- section_code: int32 [512, 16, 20], P(('gx', 'gy')), may hold values from 0 to 7, as said below
- pipe_face: int32 [512, 2, 64], P(('gx', 'gy')), may hold values from 0 to 767, as said below
- pipe_code: int32 [512, 2, 64], P(('gx', 'gy')), may hold values from 0 to 7, as said below
Outputs:
- solution_out: float32 [512, 65536], P(None, ('gx', 'gy'))
- residual_out: float32 [512, 65536], P(None, ('gx', 'gy'))
- norm_ratio: float32 [1], replicated
The draws below stay inside these ranges and needn't reach their ends.
Inputs may be any that keep to these rules, and one draw needn't show every extreme that they name: `elem_live`: one device holds all 128 slots in every draw. A face id 6 e + f names face f of slot e of the device, with e below the device's elem_live; no id appears twice on a device over section_face and pipe_face; -1 marks an empty slot, and in each peer's row the slots holding faces come first. Slot (q, c) of device (x, y) holds a face exactly when slot (y, c) of device (x, q) does; in the row q = y they come in pairs (c, c xor 1). Each device's rows for peers y - 1, y + 1 and y + 16 / 2 (mod 16) are full; rows for other peers more than two places away (mod 16) are empty. `section_code`: with inv(o) = o for o < 4 and 4 + 2 (o mod 2) + floor((o mod 4) / 2) for o >= 4, the codes of two paired slots are inv of each other; empty slots hold 0. `pipe_face`: every slot holds a face, as for section_face. `pipe_code`: the codes of two paired slots are inv of each other, as for section_code. `coarse_inverse`: Symmetric.
All inputs are finite; a program needn't handle non-finite values.
Results may differ from the reference program's by a relative error of at most 0.0003.
Values sent between devices are 32-bit elements; how exact they have to be, the bound alone decides.
A program may use at most 64 MiB of HBM per device.

```python
import math
import jax
import jax.numpy as jnp
from jax import lax

EDGE = 8
NPTS = 512
E_DEV = 128
CAP_S = 20
CAP_P = 64
NE = 65536
NV = 8192
N_GX = 32
N_GY = 16


def invert_codes(orient_codes):
    return jnp.where(orient_codes >= 4, 4 + 2 * (orient_codes % 2) + orient_codes % 4 // 2, orient_codes)


def face_layout(key):
    base_key = jax.random.fold_in(key, 7)
    device_total = N_GX * N_GY
    key_list = [jax.random.fold_in(base_key, number) for number in range(6)]
    full_device = jax.random.randint(key_list[0], (), 0, device_total)
    alive_count = jax.random.randint(key_list[1], (device_total,), E_DEV * 5 // 8, E_DEV + 1)
    alive_count = jnp.where(jnp.arange(device_total) == full_device, E_DEV, alive_count).astype(jnp.int32)
    drawn_load = jax.random.randint(key_list[2], (N_GX, N_GY, N_GY), CAP_S // 3, CAP_S + 1)
    own_pos = jnp.arange(N_GY)[:, None]
    peer_pos = jnp.arange(N_GY)[None, :]
    slot_load = jnp.where(peer_pos > own_pos, drawn_load, jnp.swapaxes(drawn_load, 1, 2))
    slot_load = jnp.where(peer_pos == own_pos, 2 * (drawn_load // 2), slot_load)
    cycle_gap = jnp.minimum((peer_pos - own_pos) % N_GY, (own_pos - peer_pos) % N_GY)
    beside_pos = (cycle_gap == 1) | (cycle_gap == N_GY // 2)
    slot_load = jnp.where(beside_pos, CAP_S, slot_load)
    slot_load = jnp.where((cycle_gap <= 2) | beside_pos, slot_load, 0).reshape(device_total, N_GY)
    slot_index = jnp.arange(CAP_S)
    live_slot = slot_index[None, None, :] < slot_load[:, :, None]
    offsets = jnp.cumsum(slot_load, axis=1) - slot_load
    section_rank = jnp.minimum(offsets[:, :, None] + slot_index[None, None, :], 6 * E_DEV - 1)
    section_total = jnp.sum(slot_load, axis=1)
    pipe_rank = section_total[:, None, None] + jnp.arange(2)[None, :, None] * CAP_P + jnp.arange(CAP_P)[None, None, :]
    shuffled = jax.vmap(lambda part_key: jax.random.permutation(part_key, 6 * E_DEV))(jax.random.split(key_list[3], device_total))
    face_ids = jnp.arange(6 * E_DEV)
    dead_face = face_ids[None, :] // 6 >= alive_count[:, None]
    scores = shuffled + dead_face.astype(shuffled.dtype) * (6 * E_DEV)
    ordering = jnp.argsort(scores, axis=1, stable=True).astype(jnp.int32)
    picked = jnp.take_along_axis(ordering, section_rank.reshape(device_total, -1), axis=1).reshape(device_total, N_GY, CAP_S)
    section_face = jnp.where(live_slot, picked, -1).astype(jnp.int32)
    pipe_face = jnp.take_along_axis(ordering, pipe_rank.reshape(device_total, -1), axis=1).reshape(device_total, 2, CAP_P).astype(jnp.int32)
    orient_base = jax.random.randint(key_list[4], (N_GX, N_GY, N_GY, CAP_S), 0, 8)
    mirrored = invert_codes(jnp.swapaxes(orient_base, 1, 2))
    section_code = jnp.where((peer_pos > own_pos)[None, :, :, None], orient_base, mirrored)
    even_code = jnp.repeat(orient_base[..., 0::2], 2, axis=-1)
    self_code = jnp.where(slot_index % 2 == 0, even_code, invert_codes(even_code))
    section_code = jnp.where((peer_pos == own_pos)[None, :, :, None], self_code, section_code)
    section_code = jnp.where(live_slot, section_code.reshape(device_total, N_GY, CAP_S), 0).astype(jnp.int32)
    upward = jax.random.randint(key_list[5], (N_GX, N_GY, CAP_P), 0, 8)
    downward = invert_codes(jnp.roll(upward, 1, axis=0))
    pipe_code = jnp.stack([downward, upward], axis=2).reshape(device_total, 2, CAP_P).astype(jnp.int32)
    return (alive_count, section_face, section_code, pipe_face, pipe_code)


def draw_elem_live(key, part):
    return face_layout(key)[0]


def draw_section_face(key, part):
    return face_layout(key)[1]


def draw_section_code(key, part):
    return face_layout(key)[2]


def draw_pipe_face(key, part):
    return face_layout(key)[3]


def draw_pipe_code(key, part):
    return face_layout(key)[4]


def draw_residual(key, part):
    values = jnp.clip(jax.random.normal(jax.random.fold_in(key, 3), (NPTS, NE), jnp.float32), -4.0, 4.0)
    device = (jnp.arange(NE) // E_DEV).astype(jnp.float32)
    rising = 1.0 + 2.0 * device / max(N_GX * N_GY - 1, 1)
    return values * rising[None, :]


def draw_coarse_inverse(key, part):
    raw_values = jnp.clip(jax.random.normal(jax.random.fold_in(key, 9), (NV, NV), jnp.float32), -4.0, 4.0)
    symmetric = (raw_values + raw_values.T) * (0.7 * 0.07 / math.sqrt(NV))
    diagonal = 0.07 + 0.07 * jax.random.uniform(jax.random.fold_in(key, 10), (NV,), jnp.float32)
    return symmetric + jnp.eye(NV, dtype=jnp.float32) * diagonal[None, :]


def place_ends(drawn, own_key, smallest, high):
    shape = drawn.shape
    spot = [jax.random.randint(jax.random.fold_in(own_key, axis), (), 0, shape[axis]) for axis in range(len(shape))]
    drawn = drawn.at[tuple(spot)].set(smallest)
    longest = shape.index(max(shape))
    spot[longest] = (spot[longest] + 1) % shape[longest]
    return drawn.at[tuple(spot)].set(high)


def shard_levels(own_key, shape, cuts, smallest, top_value):
    def one(axis_at, parts):
        heights = jax.random.uniform(jax.random.fold_in(jax.random.fold_in(own_key, 6), axis_at), (parts,), jnp.float32, smallest / len(cuts), top_value / len(cuts))
        return jnp.repeat(jnp.exp(heights), shape[axis_at] // parts).reshape((-1,) + (1,) * (len(shape) - axis_at - 1))

    loudness = one(*cuts[0])
    for cut in cuts[1:]:
        loudness = loudness * one(*cut)
    return loudness


def normal_values(key, dims, deviation, bound, cuts=(), held_as=jnp.bfloat16):
    result = deviation * jax.random.normal(key, dims, jnp.float32)
    if cuts:
        result = result * shard_levels(key, dims, cuts, -0.22, 0.18)
    return jnp.clip(result, -bound, bound).astype(held_as)


def setup_inputs(seed: int = 0) -> dict:
    key_of = jax.random.split(jax.random.key(seed), 14)
    solution = normal_values(key_of[0], (NPTS, NE), 1.0, 6.0, ((1, 512),), jnp.float32)
    residual = draw_residual(jax.random.fold_in(key_of[13], 71), 0)
    metric_diag = jnp.clip(jnp.exp(math.log(0.3984375) - 2.3038113 * jax.random.uniform(key_of[2], (3, NPTS, NE), jnp.float32) ** shard_levels(key_of[2], (3, NPTS, NE), ((2, 512),), -0.2, 0.2)), 0.039794922, 0.3984375).astype(jnp.bfloat16)
    metric_cross = jnp.clip(jax.random.uniform(key_of[3], (3, NPTS, NE), jnp.float32, -0.017944336, 0.017944336) * shard_levels(key_of[3], (3, NPTS, NE), ((2, 512),), -0.4, 0.0), -0.017944336, 0.017944336).astype(jnp.bfloat16)
    fdm_vectors = normal_values(key_of[4], (3, EDGE, EDGE, NE), 0.35, 5.0, ((3, 512),), jnp.float32)
    fdm_values = jnp.clip(jnp.exp(math.log(20.0) - 5.9914645 * jax.random.uniform(key_of[5], (3, EDGE, NE), jnp.float32) ** shard_levels(key_of[5], (3, EDGE, NE), ((2, 512),), -0.2, 0.2)), 0.05, 20.0)
    vertex_ids = place_ends(jax.random.randint(key_of[6], (8, NE), 0, NV), jax.random.fold_in(key_of[6], 1), 0, NV - 1).astype(jnp.int32)
    coarse_inverse = draw_coarse_inverse(jax.random.fold_in(key_of[13], 71), 0)
    elem_live = draw_elem_live(jax.random.fold_in(key_of[13], 71), 0)
    section_face = draw_section_face(jax.random.fold_in(key_of[13], 71), 0)
    section_code = draw_section_code(jax.random.fold_in(key_of[13], 71), 0)
    pipe_face = draw_pipe_face(jax.random.fold_in(key_of[13], 71), 0)
    pipe_code = draw_pipe_code(jax.random.fold_in(key_of[13], 71), 0)
    return dict(solution=solution, residual=residual, metric_diag=metric_diag, metric_cross=metric_cross, fdm_vectors=fdm_vectors, fdm_values=fdm_values, vertex_ids=vertex_ids, coarse_inverse=coarse_inverse, elem_live=elem_live, section_face=section_face, section_code=section_code, pipe_face=pipe_face, pipe_code=pipe_code)


top_precision = lax.Precision.HIGHEST


def node_points():
    node_index = jnp.arange(EDGE).astype(jnp.float32)
    return -jnp.cos(jnp.pi * node_index / (EDGE - 1))


def derivative_matrix():
    points = node_points()
    node_index = jnp.arange(EDGE)
    weights = jnp.where((node_index == 0) | (node_index == EDGE - 1), 2.0, 1.0).astype(jnp.float32)
    parity = jnp.where((node_index[:, None] + node_index[None, :]) % 2 == 0, 1.0, -1.0).astype(jnp.float32)
    identity = jnp.eye(EDGE, dtype=jnp.float32)
    spacing = points[:, None] - points[None, :] + identity
    offdiag = (weights[:, None] / weights[None, :]) * parity / spacing * (1.0 - identity)
    return offdiag - jnp.diag(jnp.sum(offdiag, axis=1))


def corner_table():
    points = node_points()
    hat_values = jnp.stack([(1.0 - points) * 0.5, (1.0 + points) * 0.5])
    corner_weights = hat_values[:, None, None, :, None, None] * hat_values[None, :, None, None, :, None] * hat_values[None, None, :, None, None, :]
    return corner_weights.reshape(8, EDGE ** 3)


def orient_faces(face_rows, orient_codes):
    face_grid = face_rows.reshape(-1, EDGE, EDGE)
    face_grid = jnp.where((orient_codes % 2 == 1)[:, None, None], face_grid[:, ::-1, :], face_grid)
    face_grid = jnp.where(((orient_codes // 2) % 2 == 1)[:, None, None], face_grid[:, :, ::-1], face_grid)
    face_grid = jnp.where((orient_codes >= 4)[:, None, None], jnp.swapaxes(face_grid, 1, 2), face_grid)
    return face_grid.reshape(-1, EDGE * EDGE)


def face_slabs(element_cube):
    stacked = jnp.stack([element_cube[0], element_cube[EDGE - 1], element_cube[:, 0], element_cube[:, EDGE - 1], element_cube[:, :, 0], element_cube[:, :, EDGE - 1]])
    return jnp.transpose(stacked, (3, 0, 1, 2)).reshape(-1, EDGE * EDGE)


def add_slabs(element_cube, face_extra):
    face_parts = jnp.transpose(face_extra.reshape(-1, 6, EDGE, EDGE), (1, 2, 3, 0))
    element_cube = element_cube.at[0].add(face_parts[0])
    element_cube = element_cube.at[EDGE - 1].add(face_parts[1])
    element_cube = element_cube.at[:, 0].add(face_parts[2])
    element_cube = element_cube.at[:, EDGE - 1].add(face_parts[3])
    element_cube = element_cube.at[:, :, 0].add(face_parts[4])
    element_cube = element_cube.at[:, :, EDGE - 1].add(face_parts[5])
    return element_cube


def scatter_faces(face_count, targets, face_rows):
    placed = jnp.where(targets < 0, face_count, targets).astype(jnp.int32)
    return jnp.zeros((face_count, EDGE * EDGE), dtype=face_rows.dtype).at[placed].add(face_rows, mode="drop")


def fdm_solve(element_cube, vectors, values):
    spectral = jnp.einsum("iae,ijke->ajke", vectors[0], element_cube, precision=top_precision)
    spectral = jnp.einsum("jbe,ajke->abke", vectors[1], spectral, precision=top_precision)
    spectral = jnp.einsum("kce,abke->abce", vectors[2], spectral, precision=top_precision)
    eigen_sums = values[0][:, None, None, :] + values[1][None, :, None, :] + values[2][None, None, :, :]
    spectral = spectral / eigen_sums
    restored = jnp.einsum("iae,abce->ibce", vectors[0], spectral, precision=top_precision)
    restored = jnp.einsum("jbe,ibce->ijce", vectors[1], restored, precision=top_precision)
    return jnp.einsum("kce,ijce->ijke", vectors[2], restored, precision=top_precision)


def local_operator(field, diag_part, cross_part, derivative):
    element_cube = field.reshape(EDGE, EDGE, EDGE, -1)
    diagonal = diag_part.astype(jnp.float32).reshape(3, EDGE, EDGE, EDGE, -1)
    cross_terms = cross_part.astype(jnp.float32).reshape(3, EDGE, EDGE, EDGE, -1)
    grad_first = jnp.einsum("ai,ijke->ajke", derivative, element_cube, precision=top_precision)
    grad_second = jnp.einsum("aj,ijke->iake", derivative, element_cube, precision=top_precision)
    grad_third = jnp.einsum("ak,ijke->ijae", derivative, element_cube, precision=top_precision)
    flux_first = diagonal[0] * grad_first + cross_terms[0] * grad_second + cross_terms[1] * grad_third
    flux_second = cross_terms[0] * grad_first + diagonal[1] * grad_second + cross_terms[2] * grad_third
    flux_third = cross_terms[1] * grad_first + cross_terms[2] * grad_second + diagonal[2] * grad_third
    curvature = jnp.sum(grad_first * flux_first + grad_second * flux_second + grad_third * flux_third) + jnp.sum(element_cube * element_cube)
    applied = jnp.einsum("ai,ajke->ijke", derivative, flux_first, precision=top_precision)
    applied = applied + jnp.einsum("aj,iake->ijke", derivative, flux_second, precision=top_precision)
    applied = applied + jnp.einsum("ak,ijae->ijke", derivative, flux_third, precision=top_precision)
    return (applied + element_cube).reshape(EDGE ** 3, -1), curvature


def by_device(function, arrays):
    folded = tuple(jnp.moveaxis(member.reshape(member.shape[:-1] + (N_GX * N_GY, E_DEV)), -2, 0) for member in arrays)
    return lax.map(lambda grouped: function(*grouped), folded)


def unfold(member):
    return jnp.moveaxis(member, 0, -2).reshape(member.shape[1:-1] + (-1,))


def face_sum(field, section_face, section_code, pipe_face, pipe_code):
    element_cube = field.reshape(EDGE, EDGE, EDGE, -1)
    face_values = face_slabs(element_cube)
    per_device = 6 * E_DEV
    device = jnp.arange(N_GX * N_GY).astype(jnp.int32)
    row_pos = device // N_GY
    col_pos = device % N_GY
    peer_index = jnp.arange(N_GY).astype(jnp.int32)
    slot_index = jnp.arange(CAP_S).astype(jnp.int32)
    partner_dev = row_pos[:, None, None] * N_GY + peer_index[None, :, None]
    same_peer = peer_index[None, :, None] == col_pos[:, None, None]
    partner_slot = jnp.where(same_peer, slot_index[None, None, :] + 1 - 2 * (slot_index[None, None, :] % 2), slot_index[None, None, :])
    partner_face = section_face[partner_dev, col_pos[:, None, None], partner_slot]
    source = (partner_dev * per_device + jnp.maximum(partner_face, 0)).astype(jnp.int32)
    incoming = orient_faces(face_values[source.reshape(-1)], section_code.reshape(-1))
    target = jnp.where(section_face >= 0, device[:, None, None] * per_device + section_face, -1).reshape(-1).astype(jnp.int32)
    side_index = jnp.arange(2).astype(jnp.int32)
    pipe_row = (row_pos[:, None] - 1 + 2 * side_index[None, :]) % N_GX
    pipe_dev = pipe_row * N_GY + col_pos[:, None]
    pipe_partner = pipe_face[pipe_dev[:, :, None], (1 - side_index)[None, :, None], jnp.arange(CAP_P).astype(jnp.int32)[None, None, :]]
    pipe_source = (pipe_dev[:, :, None] * per_device + pipe_partner).astype(jnp.int32)
    beside = orient_faces(face_values[pipe_source.reshape(-1)], pipe_code.reshape(-1))
    pipe_target = (device[:, None, None] * per_device + pipe_face).reshape(-1).astype(jnp.int32)
    face_extra = scatter_faces(face_values.shape[0], jnp.concatenate([target, pipe_target]), jnp.concatenate([incoming, beside]))
    return add_slabs(element_cube, face_extra).reshape(EDGE ** 3, -1)


def reference(solution, residual, metric_diag, metric_cross, fdm_vectors, fdm_values, vertex_ids, coarse_inverse, elem_live, section_face, section_code, pipe_face, pipe_code):
    slot_index = jnp.arange(N_GX * N_GY * E_DEV).astype(jnp.int32)
    alive_mask = (slot_index % E_DEV < elem_live[slot_index // E_DEV]).astype(jnp.float32)
    rmask = residual * alive_mask[None, :]
    corner_weights = corner_table()
    derivative = derivative_matrix()
    corners = jnp.dot(corner_weights, rmask, precision=top_precision)
    coarse_rhs = jax.ops.segment_sum(corners.reshape(-1), vertex_ids.reshape(-1), num_segments=NV)
    coarse_sol = jnp.dot(coarse_inverse, coarse_rhs, precision=top_precision)
    smooth = unfold(by_device(lambda vectors_part, values_part, field_part: fdm_solve(field_part.reshape(EDGE, EDGE, EDGE, -1), vectors_part, values_part).reshape(EDGE ** 3, -1), (fdm_vectors, fdm_values, rmask)))
    summed = face_sum(smooth, section_face, section_code, pipe_face, pipe_code)
    lifted = jnp.dot(corner_weights.T, coarse_sol[vertex_ids], precision=top_precision)
    direction = alive_mask[None, :] * (summed + lifted)
    applied_parts, curvature_parts = by_device(lambda field_part, diag_part, cross_part: local_operator(field_part, diag_part, cross_part, derivative), (direction, metric_diag, metric_cross))
    curvature = jnp.sum(curvature_parts)
    image = face_sum(unfold(applied_parts), section_face, section_code, pipe_face, pipe_code)
    precond_dot = jnp.sum(rmask * direction)
    old_norm = jnp.sum(rmask * rmask)
    step_length = precond_dot / curvature
    solution_out = alive_mask[None, :] * (solution + step_length * direction)
    residual_out = rmask - step_length * image
    norm_ratio = jnp.sum(residual_out * residual_out) / old_norm
    return solution_out, residual_out, norm_ratio.reshape(1)
```

```python
import functools

import numpy as np
import jax
import jax.numpy as jnp
from jax import lax
from jax.experimental import pallas as pl
from jax.experimental.pallas import tpu as pltpu
from jax.sharding import PartitionSpec as P

EDGE = 8
LANES = 128
POINTS = 512
F32 = jnp.float32
BF16 = jnp.bfloat16
MESH = pl.DeviceIdType.MESH
NT = (((1,), (1,)), ((), ()))

ROWS = 320
FIRST = 32
PEER_ROW = 64
PEER_ROWS = 24
SPARE = 184
PIPE_ROW = 192
PIPE_ROWS = 64
SENT_ROWS = 5 * PEER_ROWS + 2 * PIPE_ROWS
USED = ROWS - FIRST


def node_points():
    return -np.cos(np.pi * np.arange(EDGE) / (EDGE - 1))


def derivative_matrix():
    t = node_points()
    c = np.where((np.arange(EDGE) == 0) | (np.arange(EDGE) == EDGE - 1), 2.0, 1.0)
    d = np.zeros((EDGE, EDGE))
    for a in range(EDGE):
        for b in range(EDGE):
            if a != b:
                d[a, b] = c[a] / c[b] * (-1.0) ** (a + b) / (t[a] - t[b])
    for a in range(EDGE):
        d[a, a] = -np.sum(d[a])
    return d


def halves(matrix):
    front, back = matrix[:4, :4], matrix[:4, ::-1][:, :4]
    return (front + back) / 2, (front - back) / 2


D_EVEN, D_ODD = halves(derivative_matrix())
T_EVEN, T_ODD = halves(derivative_matrix().T)
HATS = np.stack([(1.0 - node_points()) / 2, (1.0 + node_points()) / 2])


def mirrored(even, odd, u):
    total = [u[m] + u[7 - m] for m in range(4)]
    apart = [u[m] - u[7 - m] for m in range(4)]
    front, back = [], []
    for a in range(4):
        e = float(even[a, 0]) * total[0]
        o = float(odd[a, 0]) * apart[0]
        for m in range(1, 4):
            e = e + float(even[a, m]) * total[m]
            o = o + float(odd[a, m]) * apart[m]
        front.append(o + e)
        back.append(o - e)
    return front + back[::-1]


def split(x):
    high = x.astype(BF16)
    return high, (x - high.astype(F32)).astype(BF16)


def iota(shape, dim):
    return lax.broadcasted_iota(jnp.int32, shape, dim)


def kernel(
    n_x,
    n_y,
    live_ref,
    vid_ref,
    eig_ref,
    sface_ref,
    scode_ref,
    pface_ref,
    pcode_ref,
    sol_hbm,
    res_hbm,
    diag_hbm,
    cross_hbm,
    fdm_hbm,
    inv_hbm,
    sol_out,
    res_out,
    ratio_out,
    sol_in,
    rm,
    diag,
    cross,
    fdm,
    inv,
    buf_a,
    buf_b,
    field,
    turned,
    turned2,
    grad1,
    direction,
    x_one,
    y_one,
    h_one,
    part,
    rc1,
    own2,
    rc2,
    own3,
    rc3,
    own4,
    rc4,
    own5,
    rc5,
    coarse,
    idm,
    cdm,
    onehot,
    masks,
    perm,
    faces,
    out1,
    inc1,
    out2,
    inc2,
    picked,
    own_a,
    rc_a,
    own_b,
    rc_b,
    in_sem,
    send_sem,
    recv_sem,
):
    x, y = lax.axis_index("gx"), lax.axis_index("gy")
    offsets = (1, n_y - 1, 2, n_y - 2, n_y // 2)
    back_to = (1, 0, 3, 2, 4)

    loads = [
        pltpu.make_async_copy(s, d, in_sem.at[i])
        for i, (s, d) in enumerate(
            [(res_hbm, rm), (fdm_hbm, fdm), (inv_hbm, inv), (diag_hbm, diag), (cross_hbm, cross), (sol_hbm, sol_in)]
        )
    ]
    for load in loads:
        load.start()

    barrier = pltpu.get_barrier_semaphore()

    def greet(axis, me, n):
        def body(k, c):
            pl.semaphore_signal(barrier, inc=1, device_id={axis: lax.rem(me + k, n)}, device_id_type=MESH)
            return c

        lax.fori_loop(1, n, body, 0)

    greet("gy", y, n_y)
    greet("gx", x, n_x)

    def send_all(axis, me, n, source, landing, phase):
        def body(k, c):
            target = lax.rem(me + k, n)
            pltpu.make_async_remote_copy(
                src_ref=source(target),
                dst_ref=landing.at[me],
                send_sem=send_sem.at[phase],
                recv_sem=recv_sem.at[phase],
                device_id={axis: target},
                device_id_type=MESH,
            ).start()
            return c

        lax.fori_loop(1, n, body, 0)

    def await_all(sem, landing, n):
        some = landing.at[pl.ds(0, n - 1)]
        pltpu.make_async_copy(some, some, sem).wait()

    alive = (iota((1, LANES), 1) < live_ref[0]).astype(F32)
    lane = iota((1, LANES), 1)
    sub8 = iota((EDGE, 1), 0)
    hat_rows = []
    for c in range(2):
        h = jnp.zeros((EDGE, 1), F32)
        for k in range(EDGE):
            h = jnp.where(sub8 == k, float(HATS[c, k]), h)
        hat_rows.append(h)

    inc1[pl.ds(SPARE, 8), :] = jnp.zeros((8, LANES), F32)
    inc2[pl.ds(SPARE, 8), :] = jnp.zeros((8, LANES), F32)
    loads[0].wait()
    along_i = [None, None]
    for i in range(EDGE):
        slab = rm[pl.ds(64 * i, 64), :] * alive
        rm[pl.ds(64 * i, 64), :] = slab
        for c in range(2):
            term = float(HATS[c, i]) * slab
            along_i[c] = term if i == 0 else along_i[c] + term
    high_iota = iota((64, LANES), 0)
    low_iota = iota((LANES, LANES), 0)
    for ci in range(2):
        for cj in range(2):
            plane = float(HATS[cj, 0]) * along_i[ci][0:8]
            for j in range(1, EDGE):
                plane = plane + float(HATS[cj, j]) * along_i[ci][8 * j : 8 * j + 8]
            for ck in range(2):
                c = 4 * ci + 2 * cj + ck
                value = jnp.sum(plane * hat_rows[ck], axis=0, keepdims=True)
                ids = vid_ref[c : c + 1, :]
                at = pl.ds(c * LANES, LANES)
                here = (high_iota == (ids >> 7)).astype(F32)
                h_one[:, at] = here
                high, low = split(here * value)
                x_one[0:64, at] = high
                x_one[64:128, at] = low
                y_one[:, at] = (low_iota == (ids & 127)).astype(F32).astype(BF16)
    both = lax.dot_general(x_one[...], y_one[...], NT, preferred_element_type=F32)
    partial = both[0:64] + both[64:128]
    rows1 = 64 // n_y
    for q in range(n_y):
        part[q] = partial[rows1 * q : rows1 * q + rows1]

    pl.semaphore_wait(barrier, n_x + n_y - 2)

    send_all("gy", y, n_y, lambda t: part.at[t], rc1, 0)
    rc1[y] = part[y]

    def column(row, rows, swap=0):
        width = row.shape[1]
        diagonal = (iota((rows, width), 0) ^ swap) == iota((rows, width), 1)
        kept = jnp.where(diagonal, row.astype(F32) + 1.0, 0.0)
        return jnp.broadcast_to(jnp.sum(kept, axis=1, keepdims=True) - 1.0, (rows, LANES))

    idm[pl.ds(0, 32), :] = column(sface_ref[0, pl.ds(y, 1), :], 32, 1)
    idm[pl.ds(32, 32), :] = column(sface_ref[0, pl.ds(y, 1), :], 32)
    cdm[pl.ds(0, 32), :] = column(scode_ref[0, pl.ds(y, 1), :], 32)
    for g in range(5):
        peer = lax.rem(y + offsets[g], n_y)
        at = PEER_ROW + PEER_ROWS * g
        idm[pl.ds(at, PEER_ROWS), :] = column(sface_ref[0, pl.ds(peer, 1), :], PEER_ROWS)
        cdm[pl.ds(at - FIRST, PEER_ROWS), :] = column(scode_ref[0, pl.ds(peer, 1), :], PEER_ROWS)
    idm[pl.ds(SPARE, 8), :] = jnp.full((8, LANES), -1.0, F32)
    cdm[pl.ds(SPARE - FIRST, 8), :] = jnp.full((8, LANES), -1.0, F32)
    for s in range(2):
        at = PIPE_ROW + PIPE_ROWS * s
        idm[pl.ds(at, PIPE_ROWS), :] = column(pface_ref[0, s : s + 1, :], PIPE_ROWS)
        cdm[pl.ds(at - FIRST, PIPE_ROWS), :] = column(pcode_ref[0, s : s + 1, :], PIPE_ROWS)
    ids = idm[...]
    for f in range(6):
        onehot[:, pl.ds(f * LANES, LANES)] = (ids == (6 * lane + f).astype(F32)).astype(F32).astype(BF16)
    codes = cdm[...]
    half = (lane >> 6).astype(F32)
    for p in range(4):
        masks[:, pl.ds(p * LANES, LANES)] = (codes == 2.0 * p + half).astype(F32).astype(BF16)
    grid_row = iota((LANES, LANES), 0)
    grid_lane = iota((LANES, LANES), 1)
    first, second = (grid_row & 63) >> 3, grid_row & 7
    flip = 7 * (grid_lane >> 6)
    for t in range(8):
        a, b = (second, first) if t % 4 >= 2 else (first, second)
        b = b ^ 7 if t % 2 == 1 else b
        source = 8 * (a ^ flip) + b
        fits = (source == (grid_lane & 63)) & ((grid_row < 64) if t < 4 else (grid_row >= 64))
        perm[:, pl.ds(t * LANES, LANES)] = fits.astype(F32).astype(BF16)

    await_all(recv_sem.at[0], rc1, n_y)
    mine = jnp.sum(rc1[...], axis=0)
    own2[...] = mine
    rc2[x] = mine
    send_all("gx", x, n_x, lambda t: own2, rc2, 1)

    def sum_of(coef, slabs, a):
        total = coef(0, a) * slabs(0)
        for m in range(1, EDGE):
            total = total + coef(m, a) * slabs(m)
        return total

    def per_row(body):
        def step(a, c):
            body(a)
            return c

        lax.fori_loop(0, EDGE, step, 0)

    def slab_i(ref):
        return lambda m: ref[pl.ds(pl.multiple_of(64 * m, 64), 64), :]

    def slab_j(ref):
        cube = ref.reshape(EDGE, EDGE, EDGE, LANES)
        return lambda m: cube[:, m].reshape(64, LANES)

    def forward(d):
        return lambda m, a: fdm[d, m, pl.ds(a, 1), :]

    def backward(d):
        return lambda m, a: fdm[d, a, m : m + 1, :]

    def put_i(ref, a, value):
        ref[pl.ds(pl.multiple_of(64 * a, 64), 64), :] = value

    def put_j(ref, a, value):
        ref.reshape(EDGE, EDGE, EDGE, LANES)[:, pl.ds(a, 1)] = value.reshape(EDGE, 1, EDGE, LANES)

    loads[1].wait()
    per_row(lambda a: put_i(buf_a, a, sum_of(forward(0), slab_i(rm), a)))
    per_row(lambda a: put_j(buf_b, a, sum_of(forward(1), slab_j(buf_a), a)))
    for k in range(EDGE):
        turned[pl.ds(64 * k, 64), :] = buf_b[pl.ds(k, 64, stride=EDGE), :]
    base = jnp.concatenate([eig_ref[0, a : a + 1, :] + eig_ref[1] for a in range(EDGE)], axis=0)
    buf_a[pl.ds(0, 64), :] = base

    def spectral(a):
        value = sum_of(forward(2), slab_i(turned), a)
        put_i(buf_b, a, value / (buf_a[pl.ds(0, 64), :] + eig_ref[2, pl.ds(a, 1), :]))

    per_row(spectral)

    await_all(recv_sem.at[1], rc2, n_x)
    mine = jnp.sum(rc2[...], axis=0)
    own3[...] = mine
    rc3[y] = mine
    send_all("gy", y, n_y, lambda t: own3, rc3, 2)

    per_row(lambda a: put_i(turned, a, sum_of(backward(2), slab_i(buf_b), a)))
    for k in range(EDGE):
        buf_a[pl.ds(k, 64, stride=EDGE), :] = turned[pl.ds(64 * k, 64), :]
    per_row(lambda a: put_j(buf_b, a, sum_of(backward(1), slab_j(buf_a), a)))
    per_row(lambda a: put_i(field, a, sum_of(backward(0), slab_i(buf_b), a)))

    def face_of(ref, f):
        if f < 2:
            return ref[pl.ds(448 * f, 64), :]
        if f < 4:
            return slab_j(ref)(7 * (f - 2))
        return ref[pl.ds(7 * (f - 4), 64, stride=EDGE), :]

    def send_faces(ref, out, inc, phase):
        for f in range(6):
            high, low = split(face_of(ref, f))
            faces[0:64, pl.ds(f * LANES, LANES)] = high
            faces[64:128, pl.ds(f * LANES, LANES)] = low
        found = lax.dot_general(onehot[...], faces[...], NT, preferred_element_type=F32)
        found = found + pltpu.roll(found, 64, 1)
        out[...] = found
        inc[pl.ds(FIRST, 32), :] = found[0:32]
        hops = [
            (PEER_ROW + PEER_ROWS * g, PEER_ROW + PEER_ROWS * back_to[g], PEER_ROWS, {"gy": lax.rem(y + offsets[g], n_y)})
            for g in range(5)
        ] + [
            (
                PIPE_ROW + PIPE_ROWS * s,
                PIPE_ROW + PIPE_ROWS * (1 - s),
                PIPE_ROWS,
                {"gx": lax.rem(x + n_x - 1 + 2 * s, n_x)},
            )
            for s in range(2)
        ]
        for start, land, count, target in hops:
            pltpu.make_async_remote_copy(
                src_ref=out.at[pl.ds(start, count)],
                dst_ref=inc.at[pl.ds(land, count)],
                send_sem=send_sem.at[phase],
                recv_sem=recv_sem.at[phase],
                device_id=target,
                device_id_type=MESH,
            ).start()

    def await_faces(sem, inc):
        some = inc.at[pl.ds(0, SENT_ROWS)]
        pltpu.make_async_copy(some, some, sem).wait()

    def place_faces(ref, inc):
        high, low = split(inc[pl.ds(FIRST, USED), :])
        for p in range(4):
            mask = masks[:, pl.ds(p * LANES, LANES)]
            picked[:, pl.ds(p * LANES, LANES)] = high * mask
            picked[:, pl.ds((p + 4) * LANES, LANES)] = low * mask
        across = lax.dot_general(perm[...], picked[...], NT, preferred_element_type=F32)
        extra = jnp.dot(across.astype(BF16), onehot[pl.ds(FIRST, USED), :], preferred_element_type=F32)
        extra = extra[0:64] + extra[64:128]
        cube = ref.reshape(EDGE, EDGE, EDGE, LANES)
        for f in range(6):
            more = extra[:, f * LANES : (f + 1) * LANES]
            if f < 2:
                ref[pl.ds(448 * f, 64), :] += more
            elif f < 4:
                cube[:, 7 * (f - 2)] += more.reshape(EDGE, EDGE, LANES)
            else:
                at = pl.ds(7 * (f - 4), 64, stride=EDGE)
                ref[at, :] = ref[at, :] + more

    send_faces(field, out1, inc1, 7)

    await_all(recv_sem.at[2], rc3, n_y)
    loads[2].wait()

    def rows_times(q, acc):
        for r in range(rows1):
            at = pl.ds(pl.multiple_of((q * rows1 + r) * LANES, LANES), LANES)
            acc = acc + inv[:, at] * rc3[q, r : r + 1, :]
        return acc

    acc = lax.fori_loop(0, n_y, rows_times, jnp.zeros((16, LANES), F32))
    own_values = jnp.sum(acc, axis=1, keepdims=True)
    spot = iota((16, LANES), 1) == 16 * lax.rem(y, 8) + iota((16, LANES), 0)
    row = jnp.sum(jnp.where(spot, own_values, 0.0), axis=0, keepdims=True)
    own4[...] = row
    rc4[y] = row

    send_all("gy", y, n_y, lambda t: own4, rc4, 3)
    await_faces(recv_sem.at[7], inc1)
    place_faces(field, inc1)

    await_all(recv_sem.at[3], rc4, n_y)
    pair = jnp.concatenate([jnp.sum(rc4[0:8], axis=0), jnp.sum(rc4[8:16], axis=0)], axis=0)
    own5[...] = pair
    rc5[x] = pair
    send_all("gx", x, n_x, lambda t: own5, rc5, 4)
    loads[3].wait()
    loads[4].wait()
    await_all(recv_sem.at[4], rc5, n_x)
    for q in range(n_x):
        coarse[pl.ds(2 * q, 2), :] = rc5[q]

    high, low = split(coarse[...])
    at_low = jnp.dot(jnp.concatenate([high, low], axis=0), y_one[...], preferred_element_type=F32)
    corner = jnp.sum((at_low[0:64] + at_low[64:128]) * h_one[...], axis=0, keepdims=True)
    planes = []
    for ci in range(2):
        lines = []
        for cj in range(2):
            at = (4 * ci + 2 * cj) * LANES
            lines.append(hat_rows[0] * corner[:, at : at + LANES] + hat_rows[1] * corner[:, at + LANES : at + 2 * LANES])
        planes.append(
            jnp.concatenate(
                [float(HATS[0, j]) * lines[0] + float(HATS[1, j]) * lines[1] for j in range(EDGE)], axis=0
            )
        )
    for i in range(EDGE):
        at = pl.ds(64 * i, 64)
        lifted = float(HATS[0, i]) * planes[0] + float(HATS[1, i]) * planes[1]
        direction[at, :] = alive * (field[at, :] + lifted)

    def take(ref, start, stride):
        return [ref[pl.ds(pl.multiple_of(start + stride * m, 8), 8), :] for m in range(EDGE)]

    def along_first(j, c):
        result = mirrored(D_EVEN, D_ODD, take(direction, 8 * j, 64))
        for a in range(EDGE):
            grad1[pl.ds(pl.multiple_of(64 * a + 8 * j, 8), 8), :] = result[a]
        return c

    lax.fori_loop(0, EDGE, along_first, 0)

    def turn(values, ref):
        for m in range(EDGE):
            ref[pl.ds(EDGE * m, EDGE), :] = values[m]
        return [ref[pl.ds(m, EDGE, stride=EDGE), :] for m in range(EDGE)]

    def middle(i, sums):
        curve, dots = sums
        start = pl.multiple_of(64 * i, 64)
        slab = pl.ds(start, 64)
        d = take(direction, start, 8)
        across = turn(d, turned.at[pl.ds(0, 64)])
        g3 = turn(mirrored(D_EVEN, D_ODD, across), turned.at[pl.ds(64, 64)])
        g2 = mirrored(D_EVEN, D_ODD, d)
        g1 = take(grad1, start, 8)
        m = [diag[q, slab, :].astype(F32) for q in range(3)] + [cross[q, slab, :].astype(F32) for q in range(3)]
        f2, f3 = [], []
        for j in range(EDGE):
            rr, ss, tt, rs, rt, st = [q[8 * j : 8 * j + 8] for q in m]
            u = rr * g1[j] + rs * g2[j] + rt * g3[j]
            v = rs * g1[j] + ss * g2[j] + st * g3[j]
            w = rt * g1[j] + st * g2[j] + tt * g3[j]
            curve = curve + (g1[j] * u + g2[j] * v) + (g3[j] * w + d[j] * d[j])
            grad1[pl.ds(start + 8 * j, 8), :] = u
            f2.append(v)
            f3.append(w)
        dots = dots + jnp.sum((rm[slab, :] * direction[slab, :]).reshape(EDGE, EDGE, LANES), axis=0)
        b3 = turn(mirrored(T_EVEN, T_ODD, turn(f3, turned2.at[pl.ds(0, 64)])), turned2.at[pl.ds(64, 64)])
        b2 = mirrored(T_EVEN, T_ODD, f2)
        for j in range(EDGE):
            field[pl.ds(start + 8 * j, 8), :] = (b2[j] + b3[j]) + d[j]
        return curve, dots

    zero = jnp.zeros((EDGE, LANES), F32)
    curve, dots = lax.fori_loop(0, EDGE, middle, (zero, zero))

    def back_first(j, c):
        result = mirrored(T_EVEN, T_ODD, take(grad1, 8 * j, 64))
        for a in range(EDGE):
            at = pl.ds(pl.multiple_of(64 * a + 8 * j, 8), 8)
            field[at, :] = field[at, :] + result[a]
        return c

    lax.fori_loop(0, EDGE, back_first, 0)

    send_faces(field, out2, inc2, 8)

    def folded(a, b):
        return jnp.sum((a * b).reshape(POINTS // EDGE, EDGE, LANES), axis=0)

    old = folded(rm[...], rm[...])
    await_faces(recv_sem.at[8], inc2)
    place_faces(field, inc2)

    image = field[...]
    mixed = folded(rm[...], image)
    square = folded(image, image)
    sums = jnp.zeros((1, LANES), F32)
    for q, value in enumerate((dots, curve, old, mixed, square)):
        one = jnp.sum(jnp.sum(value, axis=0, keepdims=True), axis=1, keepdims=True)
        sums = jnp.where(lane == q, one, sums)
    own_a[...] = sums
    rc_a[y] = sums
    send_all("gy", y, n_y, lambda t: own_a, rc_a, 5)
    await_all(recv_sem.at[5], rc_a, n_y)
    sums = jnp.sum(rc_a[...], axis=0)
    own_b[...] = sums
    rc_b[x] = sums
    send_all("gx", x, n_x, lambda t: own_b, rc_b, 6)
    await_all(recv_sem.at[6], rc_b, n_x)
    sums = jnp.sum(rc_b[...], axis=0)

    def total(q):
        return jnp.sum(jnp.where(lane == q, sums, 0.0), axis=1, keepdims=True)

    step = total(0) / total(1)
    for i in range(EDGE):
        at = pl.ds(64 * i, 64)
        sol_out[at, :] = alive * (sol_in_value(sol_in, at, loads[5], i) + step * direction[at, :])
        res_out[at, :] = rm[at, :] - step * field[at, :]
    ratio = (total(2) - 2.0 * step * total(3) + step * step * total(4)) / total(2)
    ratio_out[0] = jnp.sum(ratio)

    for phase, (landing, n) in enumerate(
        [(rc1, n_y), (rc2, n_x), (rc3, n_y), (rc4, n_y), (rc5, n_x), (rc_a, n_y), (rc_b, n_x)]
    ):
        await_all(send_sem.at[phase], landing, n)
    await_faces(send_sem.at[7], inc1)
    await_faces(send_sem.at[8], inc2)


def sol_in_value(ref, at, load, i):
    if i == 0:
        load.wait()
    return ref[at, :]


def on_device(n_x, n_y, *args):
    (
        sol,
        res,
        diag,
        cross,
        fdm,
        eig,
        vid,
        inv,
        live,
        sface,
        scode,
        pface,
        pcode,
    ) = args
    vmem = pl.BlockSpec(memory_space=pltpu.VMEM)
    smem = pl.BlockSpec(memory_space=pltpu.SMEM)
    hbm = pl.BlockSpec(memory_space=pl.ANY)
    rows1 = 64 // n_y
    field = pltpu.VMEM((POINTS, LANES), F32)
    return pl.pallas_call(
        functools.partial(kernel, n_x, n_y),
        out_shape=(
            jax.ShapeDtypeStruct((POINTS, LANES), F32),
            jax.ShapeDtypeStruct((POINTS, LANES), F32),
            jax.ShapeDtypeStruct((1,), F32),
        ),
        in_specs=[smem] + [vmem] * 6 + [hbm] * 6,
        out_specs=(vmem, vmem, smem),
        scratch_shapes=[
            field,
            field,
            pltpu.VMEM((3, POINTS, LANES), BF16),
            pltpu.VMEM((3, POINTS, LANES), BF16),
            pltpu.VMEM((3, EDGE, EDGE, LANES), F32),
            pltpu.VMEM(inv.shape, F32),
            field,
            field,
            field,
            field,
            field,
            field,
            field,
            pltpu.VMEM((LANES, 8 * LANES), BF16),
            pltpu.VMEM((LANES, 8 * LANES), BF16),
            pltpu.VMEM((64, 8 * LANES), F32),
            pltpu.VMEM((n_y, rows1, LANES), F32),
            pltpu.VMEM((n_y, rows1, LANES), F32),
            pltpu.VMEM((rows1, LANES), F32),
            pltpu.VMEM((n_x, rows1, LANES), F32),
            pltpu.VMEM((rows1, LANES), F32),
            pltpu.VMEM((n_y, rows1, LANES), F32),
            pltpu.VMEM((1, LANES), F32),
            pltpu.VMEM((n_y, 1, LANES), F32),
            pltpu.VMEM((2, LANES), F32),
            pltpu.VMEM((n_x, 2, LANES), F32),
            pltpu.VMEM((64, LANES), F32),
            pltpu.VMEM((ROWS, LANES), F32),
            pltpu.VMEM((USED, LANES), F32),
            pltpu.VMEM((ROWS, 6 * LANES), BF16),
            pltpu.VMEM((USED, 4 * LANES), BF16),
            pltpu.VMEM((LANES, 8 * LANES), BF16),
            pltpu.VMEM((LANES, 6 * LANES), BF16),
            pltpu.VMEM((ROWS, LANES), F32),
            pltpu.VMEM((ROWS, LANES), F32),
            pltpu.VMEM((ROWS, LANES), F32),
            pltpu.VMEM((ROWS, LANES), F32),
            pltpu.VMEM((USED, 8 * LANES), BF16),
            pltpu.VMEM((1, LANES), F32),
            pltpu.VMEM((n_y, 1, LANES), F32),
            pltpu.VMEM((1, LANES), F32),
            pltpu.VMEM((n_x, 1, LANES), F32),
            pltpu.SemaphoreType.DMA((6,)),
            pltpu.SemaphoreType.DMA((9,)),
            pltpu.SemaphoreType.DMA((9,)),
        ],
        compiler_params=pltpu.CompilerParams(
            collective_id=0, has_side_effects=True, vmem_limit_bytes=32 * 1024 * 1024
        ),
    )(live, vid, eig, sface, scode, pface, pcode, sol, res, diag, cross, fdm, inv)


def solution(mesh):
    both = ("gx", "gy")
    placed = (
        P(None, both),
        P(None, both),
        P(None, None, both),
        P(None, None, both),
        P(None, None, None, both),
        P(None, None, both),
        P(None, both),
        P(both, None),
        P(both),
        P(both, None, None),
        P(both, None, None),
        P(both, None, None),
        P(both, None, None),
    )
    return jax.shard_map(
        functools.partial(on_device, mesh.shape["gx"], mesh.shape["gy"]),
        mesh=mesh,
        in_specs=placed,
        out_specs=(P(None, both), P(None, both), P()),
        check_vma=False,
    )
```

```python
import functools

import numpy as np
import jax
import jax.numpy as jnp
from jax import lax
from jax.experimental import pallas as pl
from jax.experimental.pallas import tpu as pltpu
from jax.sharding import PartitionSpec as P

EDGE = 8
LANES = 128
POINTS = 512
F32 = jnp.float32
BF16 = jnp.bfloat16
MESH = pl.DeviceIdType.MESH
NT = (((1,), (1,)), ((), ()))

ROWS = 320
FIRST = 32
PEER_ROW = 64
PEER_ROWS = 24
SPARE = 184
PIPE_ROW = 192
PIPE_ROWS = 64
SENT_ROWS = 5 * PEER_ROWS + 2 * PIPE_ROWS
USED = ROWS - FIRST


def node_points():
    return -np.cos(np.pi * np.arange(EDGE) / (EDGE - 1))


def derivative_matrix():
    t = node_points()
    c = np.where((np.arange(EDGE) == 0) | (np.arange(EDGE) == EDGE - 1), 2.0, 1.0)
    d = np.zeros((EDGE, EDGE))
    for a in range(EDGE):
        for b in range(EDGE):
            if a != b:
                d[a, b] = c[a] / c[b] * (-1.0) ** (a + b) / (t[a] - t[b])
    for a in range(EDGE):
        d[a, a] = -np.sum(d[a])
    return d


def halves(matrix):
    front, back = matrix[:4, :4], matrix[:4, ::-1][:, :4]
    return (front + back) / 2, (front - back) / 2


D_EVEN, D_ODD = halves(derivative_matrix())
T_EVEN, T_ODD = halves(derivative_matrix().T)
HATS = np.stack([(1.0 - node_points()) / 2, (1.0 + node_points()) / 2])


def mirrored(even, odd, u):
    total = [u[m] + u[7 - m] for m in range(4)]
    apart = [u[m] - u[7 - m] for m in range(4)]
    front, back = [], []
    for a in range(4):
        e = float(even[a, 0]) * total[0]
        o = float(odd[a, 0]) * apart[0]
        for m in range(1, 4):
            e = e + float(even[a, m]) * total[m]
            o = o + float(odd[a, m]) * apart[m]
        front.append(o + e)
        back.append(o - e)
    return front + back[::-1]


def split(x):
    high = x.astype(BF16)
    return high, (x - high.astype(F32)).astype(BF16)


def iota(shape, dim):
    return lax.broadcasted_iota(jnp.int32, shape, dim)


def kernel(
    n_x,
    n_y,
    sol_hbm,
    res_hbm,
    diag_hbm,
    cross_hbm,
    fdm_hbm,
    eig_hbm,
    vid_hbm,
    inv_hbm,
    live_hbm,
    sface_hbm,
    scode_hbm,
    pface_hbm,
    pcode_hbm,
    sol_out,
    res_out,
    ratio_out,
    live_ref,
    vid_ref,
    eig_ref,
    sface_ref,
    scode_ref,
    pface_ref,
    pcode_ref,
    sol_in,
    rm,
    diag,
    cross,
    fdm,
    block,
    blocks,
    buf_a,
    buf_b,
    field,
    turned,
    turned2,
    grad1,
    direction,
    x_one,
    y_one,
    h_one,
    part,
    rc1,
    own2,
    rc2,
    own3,
    rc3,
    own4,
    rc4,
    coarse,
    idm,
    cdm,
    onehot,
    masks,
    perm,
    faces,
    out1,
    inc1,
    out2,
    inc2,
    picked,
    own_a,
    rc_a,
    own_b,
    rc_b,
    in_sem,
    out_sem,
    send_sem,
    recv_sem,
):
    x, y = lax.axis_index("gx"), lax.axis_index("gy")
    z, core = x // 2, lax.rem(x, 2)
    n_z, n_p = n_x // 2, 2 * n_y
    me = core * n_y + y
    offsets = (1, n_y - 1, 2, n_y - 2, n_y // 2)
    back_to = (1, 0, 3, 2, 4)

    moved = dict(
        live=(live_hbm, live_ref),
        residual=(res_hbm, rm),
        vid=(vid_hbm, vid_ref),
        sface=(sface_hbm, sface_ref),
        scode=(scode_hbm, scode_ref),
        pface=(pface_hbm, pface_ref),
        pcode=(pcode_hbm, pcode_ref),
        fdm=(fdm_hbm, fdm),
        eig=(eig_hbm, eig_ref),
        diag=(diag_hbm, diag),
        cross=(cross_hbm, cross),
        sol=(sol_hbm, sol_in),
    )
    loads = {n: pltpu.make_async_copy(s, d, in_sem.at[i]) for i, (n, (s, d)) in enumerate(moved.items())}
    for load in loads.values():
        load.start()

    barrier = pltpu.get_barrier_semaphore()

    def in_plane(t):
        return (2 * z + t // n_y, lax.rem(t, n_y))

    def in_line(t):
        return (2 * t + core, y)

    def greet(where, own, n):
        def body(k, c):
            pl.semaphore_signal(barrier, inc=1, device_id=where(lax.rem(own + k, n)), device_id_type=MESH)
            return c

        lax.fori_loop(1, n, body, 0)

    greet(in_plane, me, n_p)
    greet(in_line, z, n_z)
    beside = lax.rem(x + n_x - 1 + 2 * core, n_x)
    pl.semaphore_signal(barrier, inc=1, device_id=(beside, y), device_id_type=MESH)

    sent = []

    def send_all(where, own, n, source, landing, phase):
        def body(k, c):
            target = lax.rem(own + k, n)
            pltpu.make_async_remote_copy(
                src_ref=source(target),
                dst_ref=landing.at[own],
                send_sem=send_sem.at[phase],
                recv_sem=recv_sem.at[phase],
                device_id=where(target),
                device_id_type=MESH,
            ).start()
            return c

        lax.fori_loop(1, n, body, 0)
        sent.append((phase, landing.at[pl.ds(0, n - 1)]))

    def await_all(phase, landing, n):
        some = landing.at[pl.ds(0, n - 1)]
        pltpu.make_async_copy(some, some, recv_sem.at[phase]).wait()

    loads["live"].wait()
    alive = (iota((1, LANES), 1) < live_ref[0]).astype(F32)
    lane = iota((1, LANES), 1)
    sub8 = iota((EDGE, 1), 0)
    hat_rows = []
    for c in range(2):
        h = jnp.zeros((EDGE, 1), F32)
        for k in range(EDGE):
            h = jnp.where(sub8 == k, float(HATS[c, k]), h)
        hat_rows.append(h)

    inc1[pl.ds(SPARE, 8), :] = jnp.zeros((8, LANES), F32)
    inc2[pl.ds(SPARE, 8), :] = jnp.zeros((8, LANES), F32)
    loads["residual"].wait()
    loads["vid"].wait()
    along_i = [None, None]
    for i in range(EDGE):
        slab = rm[pl.ds(64 * i, 64), :] * alive
        rm[pl.ds(64 * i, 64), :] = slab
        for c in range(2):
            term = float(HATS[c, i]) * slab
            along_i[c] = term if i == 0 else along_i[c] + term
    high_iota = iota((64, LANES), 0)
    low_iota = iota((LANES, LANES), 0)
    for ci in range(2):
        for cj in range(2):
            plane = float(HATS[cj, 0]) * along_i[ci][0:8]
            for j in range(1, EDGE):
                plane = plane + float(HATS[cj, j]) * along_i[ci][8 * j : 8 * j + 8]
            for ck in range(2):
                c = 4 * ci + 2 * cj + ck
                value = jnp.sum(plane * hat_rows[ck], axis=0, keepdims=True)
                ids = vid_ref[c : c + 1, :]
                at = pl.ds(c * LANES, LANES)
                here = (high_iota == (ids >> 7)).astype(F32)
                h_one[:, at] = here
                high, low = split(here * value)
                x_one[0:64, at] = high
                x_one[64:128, at] = low
                y_one[:, at] = (low_iota == (ids & 127)).astype(F32).astype(BF16)
    both = lax.dot_general(x_one[...], y_one[...], NT, preferred_element_type=F32)
    partial = both[0:64] + both[64:128]
    for q in range(n_p):
        part[q] = partial[2 * q : 2 * q + 2]

    pl.semaphore_wait(barrier, n_p + n_z - 1)

    send_all(in_plane, me, n_p, lambda t: part.at[t], rc1, 0)
    rc1[me] = part[me]
    send_all(in_plane, me, n_p, lambda t: inv_hbm.at[:, pl.ds(pl.multiple_of(256 * t, 256), 256)], block, 9)
    keep = pltpu.make_async_copy(inv_hbm.at[:, pl.ds(pl.multiple_of(256 * me, 256), 256)], block.at[me], in_sem.at[12])
    keep.start()

    def column(row, rows, swap=0):
        width = row.shape[1]
        diagonal = (iota((rows, width), 0) ^ swap) == iota((rows, width), 1)
        kept = jnp.where(diagonal, row.astype(F32) + 1.0, 0.0)
        return jnp.broadcast_to(jnp.sum(kept, axis=1, keepdims=True) - 1.0, (rows, LANES))

    for name in ("sface", "scode", "pface", "pcode"):
        loads[name].wait()
    idm[pl.ds(0, 32), :] = column(sface_ref[0, pl.ds(y, 1), :], 32, 1)
    idm[pl.ds(32, 32), :] = column(sface_ref[0, pl.ds(y, 1), :], 32)
    cdm[pl.ds(0, 32), :] = column(scode_ref[0, pl.ds(y, 1), :], 32)
    for g in range(5):
        peer = lax.rem(y + offsets[g], n_y)
        at = PEER_ROW + PEER_ROWS * g
        idm[pl.ds(at, PEER_ROWS), :] = column(sface_ref[0, pl.ds(peer, 1), :], PEER_ROWS)
        cdm[pl.ds(at - FIRST, PEER_ROWS), :] = column(scode_ref[0, pl.ds(peer, 1), :], PEER_ROWS)
    idm[pl.ds(SPARE, 8), :] = jnp.full((8, LANES), -1.0, F32)
    cdm[pl.ds(SPARE - FIRST, 8), :] = jnp.full((8, LANES), -1.0, F32)
    for s in range(2):
        at = PIPE_ROW + PIPE_ROWS * s
        idm[pl.ds(at, PIPE_ROWS), :] = column(pface_ref[0, s : s + 1, :], PIPE_ROWS)
        cdm[pl.ds(at - FIRST, PIPE_ROWS), :] = column(pcode_ref[0, s : s + 1, :], PIPE_ROWS)
    ids = idm[...]
    for f in range(6):
        onehot[:, pl.ds(f * LANES, LANES)] = (ids == (6 * lane + f).astype(F32)).astype(F32).astype(BF16)
    codes = cdm[...]
    half = (lane >> 6).astype(F32)
    for p in range(4):
        masks[:, pl.ds(p * LANES, LANES)] = (codes == 2.0 * p + half).astype(F32).astype(BF16)
    grid_row = iota((LANES, LANES), 0)
    grid_lane = iota((LANES, LANES), 1)
    first, second = (grid_row & 63) >> 3, grid_row & 7
    flip = 7 * (grid_lane >> 6)
    for t in range(8):
        a, b = (second, first) if t % 4 >= 2 else (first, second)
        b = b ^ 7 if t % 2 == 1 else b
        source = 8 * (a ^ flip) + b
        fits = (source == (grid_lane & 63)) & ((grid_row < 64) if t < 4 else (grid_row >= 64))
        perm[:, pl.ds(t * LANES, LANES)] = fits.astype(F32).astype(BF16)

    await_all(0, rc1, n_p)
    mine = jnp.sum(rc1[...], axis=0)
    own2[...] = mine
    rc2[z] = mine
    send_all(in_line, z, n_z, lambda t: own2, rc2, 1)

    def sum_of(coef, slabs, a):
        total = coef(0, a) * slabs(0)
        for m in range(1, EDGE):
            total = total + coef(m, a) * slabs(m)
        return total

    def per_row(body):
        def step(a, c):
            body(a)
            return c

        lax.fori_loop(0, EDGE, step, 0)

    def slab_i(ref):
        return lambda m: ref[pl.ds(pl.multiple_of(64 * m, 64), 64), :]

    def slab_j(ref):
        cube = ref.reshape(EDGE, EDGE, EDGE, LANES)
        return lambda m: cube[:, m].reshape(64, LANES)

    def forward(d):
        return lambda m, a: fdm[d, m, pl.ds(a, 1), :]

    def backward(d):
        return lambda m, a: fdm[d, a, m : m + 1, :]

    def put_i(ref, a, value):
        ref[pl.ds(pl.multiple_of(64 * a, 64), 64), :] = value

    def put_j(ref, a, value):
        ref.reshape(EDGE, EDGE, EDGE, LANES)[:, pl.ds(a, 1)] = value.reshape(EDGE, 1, EDGE, LANES)

    loads["fdm"].wait()
    loads["eig"].wait()
    per_row(lambda a: put_i(buf_a, a, sum_of(forward(0), slab_i(rm), a)))
    per_row(lambda a: put_j(buf_b, a, sum_of(forward(1), slab_j(buf_a), a)))
    for k in range(EDGE):
        turned[pl.ds(64 * k, 64), :] = buf_b[pl.ds(k, 64, stride=EDGE), :]
    base = jnp.concatenate([eig_ref[0, a : a + 1, :] + eig_ref[1] for a in range(EDGE)], axis=0)
    buf_a[pl.ds(0, 64), :] = base

    def spectral(a):
        value = sum_of(forward(2), slab_i(turned), a)
        put_i(buf_b, a, value / (buf_a[pl.ds(0, 64), :] + eig_ref[2, pl.ds(a, 1), :]))

    per_row(spectral)

    per_row(lambda a: put_i(turned, a, sum_of(backward(2), slab_i(buf_b), a)))
    for k in range(EDGE):
        buf_a[pl.ds(k, 64, stride=EDGE), :] = turned[pl.ds(64 * k, 64), :]
    per_row(lambda a: put_j(buf_b, a, sum_of(backward(1), slab_j(buf_a), a)))
    per_row(lambda a: put_i(field, a, sum_of(backward(0), slab_i(buf_b), a)))

    def face_of(ref, f):
        if f < 2:
            return ref[pl.ds(448 * f, 64), :]
        if f < 4:
            return slab_j(ref)(7 * (f - 2))
        return ref[pl.ds(7 * (f - 4), 64, stride=EDGE), :]

    def send_faces(ref, out, inc, phase):
        for f in range(6):
            high, low = split(face_of(ref, f))
            faces[0:64, pl.ds(f * LANES, LANES)] = high
            faces[64:128, pl.ds(f * LANES, LANES)] = low
        found = lax.dot_general(onehot[...], faces[...], NT, preferred_element_type=F32)
        found = found + pltpu.roll(found, 64, 1)
        out[...] = found
        inc[pl.ds(FIRST, 32), :] = found[0:32]
        hops = [
            (PEER_ROW + PEER_ROWS * g, PEER_ROW + PEER_ROWS * back_to[g], PEER_ROWS, {"gy": lax.rem(y + offsets[g], n_y)})
            for g in range(5)
        ] + [
            (
                PIPE_ROW + PIPE_ROWS * s,
                PIPE_ROW + PIPE_ROWS * (1 - s),
                PIPE_ROWS,
                {"gx": lax.rem(x + n_x - 1 + 2 * s, n_x)},
            )
            for s in range(2)
        ]
        for start, land, count, target in hops:
            pltpu.make_async_remote_copy(
                src_ref=out.at[pl.ds(start, count)],
                dst_ref=inc.at[pl.ds(land, count)],
                send_sem=send_sem.at[phase],
                recv_sem=recv_sem.at[phase],
                device_id=target,
                device_id_type=MESH,
            ).start()
        sent.append((phase, inc.at[pl.ds(0, SENT_ROWS)]))

    def await_faces(phase, inc):
        some = inc.at[pl.ds(0, SENT_ROWS)]
        pltpu.make_async_copy(some, some, recv_sem.at[phase]).wait()

    def place_faces(ref, inc):
        high, low = split(inc[pl.ds(FIRST, USED), :])
        for p in range(4):
            mask = masks[:, pl.ds(p * LANES, LANES)]
            picked[:, pl.ds(p * LANES, LANES)] = high * mask
            picked[:, pl.ds((p + 4) * LANES, LANES)] = low * mask
        across = lax.dot_general(perm[...], picked[...], NT, preferred_element_type=F32)
        extra = jnp.dot(across.astype(BF16), onehot[pl.ds(FIRST, USED), :], preferred_element_type=F32)
        extra = extra[0:64] + extra[64:128]
        cube = ref.reshape(EDGE, EDGE, EDGE, LANES)
        for f in range(6):
            more = extra[:, f * LANES : (f + 1) * LANES]
            if f < 2:
                ref[pl.ds(448 * f, 64), :] += more
            elif f < 4:
                cube[:, 7 * (f - 2)] += more.reshape(EDGE, EDGE, LANES)
            else:
                at = pl.ds(7 * (f - 4), 64, stride=EDGE)
                ref[at, :] = ref[at, :] + more

    await_all(9, block, n_p)
    keep.wait()
    for n in range(n_p):
        high, low = split(block[n])
        blocks[16 * n : 16 * n + 16, :] = high
        blocks[16 * (n_p + n) : 16 * (n_p + n) + 16, :] = low

    await_all(1, rc2, n_z)
    mine = jnp.sum(rc2[...], axis=0)
    high, low = split(jnp.concatenate([mine[0:1], mine[1:2]], axis=1))
    pair = jnp.concatenate([high.astype(F32), low.astype(F32), jnp.zeros((14, 2 * LANES), F32)], axis=0).astype(BF16)
    product = lax.dot_general(pair, blocks[...], NT, preferred_element_type=F32)
    count = 16 * n_p
    product = product[0:1, :count] + (product[1:2, :count] + product[0:1, count:])
    mine = jnp.concatenate([product[:, LANES * h : LANES * h + LANES] for h in range(4)], axis=0)
    own3[...] = mine
    rc3[me] = mine
    send_all(in_plane, me, n_p, lambda t: own3, rc3, 2)

    send_faces(field, out1, inc1, 7)

    await_all(2, rc3, n_p)
    mine = jnp.sum(rc3[...], axis=0)
    own4[...] = mine
    rc4[z] = mine
    send_all(in_line, z, n_z, lambda t: own4, rc4, 3)
    await_faces(7, inc1)
    place_faces(field, inc1)
    loads["diag"].wait()
    loads["cross"].wait()

    await_all(3, rc4, n_z)
    for q in range(n_z):
        coarse[pl.ds(4 * q, 4), :] = rc4[q]

    high, low = split(coarse[...])
    at_low = jnp.dot(jnp.concatenate([high, low], axis=0), y_one[...], preferred_element_type=F32)
    corner = jnp.sum((at_low[0:64] + at_low[64:128]) * h_one[...], axis=0, keepdims=True)
    planes = []
    for ci in range(2):
        lines = []
        for cj in range(2):
            at = (4 * ci + 2 * cj) * LANES
            lines.append(hat_rows[0] * corner[:, at : at + LANES] + hat_rows[1] * corner[:, at + LANES : at + 2 * LANES])
        planes.append(
            jnp.concatenate(
                [float(HATS[0, j]) * lines[0] + float(HATS[1, j]) * lines[1] for j in range(EDGE)], axis=0
            )
        )
    for i in range(EDGE):
        at = pl.ds(64 * i, 64)
        lifted = float(HATS[0, i]) * planes[0] + float(HATS[1, i]) * planes[1]
        direction[at, :] = alive * (field[at, :] + lifted)

    def take(ref, start, stride):
        return [ref[pl.ds(pl.multiple_of(start + stride * m, 8), 8), :] for m in range(EDGE)]

    def along_first(j, c):
        result = mirrored(D_EVEN, D_ODD, take(direction, 8 * j, 64))
        for a in range(EDGE):
            grad1[pl.ds(pl.multiple_of(64 * a + 8 * j, 8), 8), :] = result[a]
        return c

    lax.fori_loop(0, EDGE, along_first, 0)

    def turn(values, ref):
        for m in range(EDGE):
            ref[pl.ds(EDGE * m, EDGE), :] = values[m]
        return [ref[pl.ds(m, EDGE, stride=EDGE), :] for m in range(EDGE)]

    def middle(i, sums):
        curve, dots = sums
        start = pl.multiple_of(64 * i, 64)
        slab = pl.ds(start, 64)
        d = take(direction, start, 8)
        across = turn(d, turned.at[pl.ds(0, 64)])
        g3 = turn(mirrored(D_EVEN, D_ODD, across), turned.at[pl.ds(64, 64)])
        g2 = mirrored(D_EVEN, D_ODD, d)
        g1 = take(grad1, start, 8)
        m = [diag[q, slab, :].astype(F32) for q in range(3)] + [cross[q, slab, :].astype(F32) for q in range(3)]
        f2, f3 = [], []
        for j in range(EDGE):
            rr, ss, tt, rs, rt, st = [q[8 * j : 8 * j + 8] for q in m]
            u = rr * g1[j] + rs * g2[j] + rt * g3[j]
            v = rs * g1[j] + ss * g2[j] + st * g3[j]
            w = rt * g1[j] + st * g2[j] + tt * g3[j]
            curve = curve + (g1[j] * u + g2[j] * v) + (g3[j] * w + d[j] * d[j])
            grad1[pl.ds(start + 8 * j, 8), :] = u
            f2.append(v)
            f3.append(w)
        dots = dots + jnp.sum((rm[slab, :] * direction[slab, :]).reshape(EDGE, EDGE, LANES), axis=0)
        b3 = turn(mirrored(T_EVEN, T_ODD, turn(f3, turned2.at[pl.ds(0, 64)])), turned2.at[pl.ds(64, 64)])
        b2 = mirrored(T_EVEN, T_ODD, f2)
        for j in range(EDGE):
            field[pl.ds(start + 8 * j, 8), :] = (b2[j] + b3[j]) + d[j]
        return curve, dots

    zero = jnp.zeros((EDGE, LANES), F32)
    curve, dots = lax.fori_loop(0, EDGE, middle, (zero, zero))

    def back_first(j, c):
        result = mirrored(T_EVEN, T_ODD, take(grad1, 8 * j, 64))
        for a in range(EDGE):
            at = pl.ds(pl.multiple_of(64 * a + 8 * j, 8), 8)
            field[at, :] = field[at, :] + result[a]
        return c

    lax.fori_loop(0, EDGE, back_first, 0)

    send_faces(field, out2, inc2, 8)

    def folded(a, b):
        return jnp.sum((a * b).reshape(POINTS // EDGE, EDGE, LANES), axis=0)

    old = folded(rm[...], rm[...])
    await_faces(8, inc2)
    place_faces(field, inc2)

    image = field[...]
    mixed = folded(rm[...], image)
    square = folded(image, image)
    sums = jnp.zeros((1, LANES), F32)
    for q, value in enumerate((dots, curve, old, mixed, square)):
        one = jnp.sum(jnp.sum(value, axis=0, keepdims=True), axis=1, keepdims=True)
        sums = jnp.where(lane == q, one, sums)
    own_a[...] = sums
    rc_a[me] = sums
    send_all(in_plane, me, n_p, lambda t: own_a, rc_a, 5)
    await_all(5, rc_a, n_p)
    sums = jnp.sum(rc_a[...], axis=0)
    own_b[...] = sums
    rc_b[z] = sums
    send_all(in_line, z, n_z, lambda t: own_b, rc_b, 6)
    await_all(6, rc_b, n_z)
    sums = jnp.sum(rc_b[...], axis=0)

    def total(q):
        return jnp.sum(jnp.where(lane == q, sums, 0.0), axis=1, keepdims=True)

    step = total(0) / total(1)
    stores = []
    loads["sol"].wait()
    for i in range(EDGE):
        at = pl.ds(64 * i, 64)
        sol_in[at, :] = alive * (sol_in[at, :] + step * direction[at, :])
        rm[at, :] = rm[at, :] - step * field[at, :]
        if i % 4 == 3:
            at = pl.ds(64 * (i - 3), 256)
            for q, (source, target) in enumerate(((sol_in, sol_out), (rm, res_out))):
                store = pltpu.make_async_copy(source.at[at], target.at[at], out_sem.at[q, i // 4])
                store.start()
                stores.append(store)
    ratio = (total(2) - 2.0 * step * total(3) + step * step * total(4)) / total(2)
    ratio_out[0] = jnp.sum(ratio)

    for phase, some in sent:
        pltpu.make_async_copy(some, some, send_sem.at[phase]).wait()
    for store in stores:
        store.wait()


def on_device(n_x, n_y, *args):
    live, vid, eig, sface, scode, pface, pcode = (args[i] for i in (8, 6, 5, 9, 10, 11, 12))
    smem = pl.BlockSpec(memory_space=pltpu.SMEM)
    hbm = pl.BlockSpec(memory_space=pl.ANY)
    n_p, n_z = 2 * n_y, n_x // 2
    field = pltpu.VMEM((POINTS, LANES), F32)
    return pl.pallas_call(
        functools.partial(kernel, n_x, n_y),
        out_shape=(
            jax.ShapeDtypeStruct((POINTS, LANES), F32),
            jax.ShapeDtypeStruct((POINTS, LANES), F32),
            jax.ShapeDtypeStruct((1,), F32),
        ),
        in_specs=[hbm] * len(args),
        out_specs=(hbm, hbm, smem),
        scratch_shapes=[
            pltpu.SMEM((1,), jnp.int32),
            pltpu.VMEM(vid.shape, jnp.int32),
            pltpu.VMEM(eig.shape, F32),
            pltpu.VMEM(sface.shape, jnp.int32),
            pltpu.VMEM(scode.shape, jnp.int32),
            pltpu.VMEM(pface.shape, jnp.int32),
            pltpu.VMEM(pcode.shape, jnp.int32),
            field,
            field,
            pltpu.VMEM((3, POINTS, LANES), BF16),
            pltpu.VMEM((3, POINTS, LANES), BF16),
            pltpu.VMEM((3, EDGE, EDGE, LANES), F32),
            pltpu.VMEM((n_p, 16, 2 * LANES), F32),
            pltpu.VMEM((32 * n_p, 2 * LANES), BF16),
            field,
            field,
            field,
            field,
            field,
            field,
            field,
            pltpu.VMEM((LANES, 8 * LANES), BF16),
            pltpu.VMEM((LANES, 8 * LANES), BF16),
            pltpu.VMEM((64, 8 * LANES), F32),
            pltpu.VMEM((n_p, 2, LANES), F32),
            pltpu.VMEM((n_p, 2, LANES), F32),
            pltpu.VMEM((2, LANES), F32),
            pltpu.VMEM((n_z, 2, LANES), F32),
            pltpu.VMEM((4, LANES), F32),
            pltpu.VMEM((n_p, 4, LANES), F32),
            pltpu.VMEM((4, LANES), F32),
            pltpu.VMEM((n_z, 4, LANES), F32),
            pltpu.VMEM((64, LANES), F32),
            pltpu.VMEM((ROWS, LANES), F32),
            pltpu.VMEM((USED, LANES), F32),
            pltpu.VMEM((ROWS, 6 * LANES), BF16),
            pltpu.VMEM((USED, 4 * LANES), BF16),
            pltpu.VMEM((LANES, 8 * LANES), BF16),
            pltpu.VMEM((LANES, 6 * LANES), BF16),
            pltpu.VMEM((ROWS, LANES), F32),
            pltpu.VMEM((ROWS, LANES), F32),
            pltpu.VMEM((ROWS, LANES), F32),
            pltpu.VMEM((ROWS, LANES), F32),
            pltpu.VMEM((USED, 8 * LANES), BF16),
            pltpu.VMEM((1, LANES), F32),
            pltpu.VMEM((n_p, 1, LANES), F32),
            pltpu.VMEM((1, LANES), F32),
            pltpu.VMEM((n_z, 1, LANES), F32),
            pltpu.SemaphoreType.DMA((13,)),
            pltpu.SemaphoreType.DMA((2, 2)),
            pltpu.SemaphoreType.DMA((10,)),
            pltpu.SemaphoreType.DMA((10,)),
        ],
        compiler_params=pltpu.CompilerParams(
            collective_id=0, has_side_effects=True, vmem_limit_bytes=60 * 1024 * 1024
        ),
    )(*args)


def solution(mesh):
    both = ("gx", "gy")
    placed = (
        P(None, both),
        P(None, both),
        P(None, None, both),
        P(None, None, both),
        P(None, None, None, both),
        P(None, None, both),
        P(None, both),
        P(both, None),
        P(both),
        P(both, None, None),
        P(both, None, None),
        P(both, None, None),
        P(both, None, None),
    )
    return jax.shard_map(
        functools.partial(on_device, mesh.shape["gx"], mesh.shape["gy"]),
        mesh=mesh,
        in_specs=placed,
        out_specs=(P(None, both), P(None, both), P()),
        check_vma=False,
    )
```

```python
import functools

import numpy as np
import jax
import jax.numpy as jnp
from jax import lax
from jax.experimental import pallas as pl
from jax.experimental.pallas import tpu as pltpu
from jax.sharding import PartitionSpec as P

EDGE = 8
LANES = 128
POINTS = 512
F32 = jnp.float32
BF16 = jnp.bfloat16
MESH = pl.DeviceIdType.MESH
NT = (((1,), (1,)), ((), ()))

ROWS = 320
FIRST = 32
PEER_ROW = 64
PEER_ROWS = 24
SPARE = 184
PIPE_ROW = 192
PIPE_ROWS = 64
SENT_ROWS = 5 * PEER_ROWS + 2 * PIPE_ROWS
USED = ROWS - FIRST


def node_points():
    return -np.cos(np.pi * np.arange(EDGE) / (EDGE - 1))


def derivative_matrix():
    t = node_points()
    c = np.where((np.arange(EDGE) == 0) | (np.arange(EDGE) == EDGE - 1), 2.0, 1.0)
    d = np.zeros((EDGE, EDGE))
    for a in range(EDGE):
        for b in range(EDGE):
            if a != b:
                d[a, b] = c[a] / c[b] * (-1.0) ** (a + b) / (t[a] - t[b])
    for a in range(EDGE):
        d[a, a] = -np.sum(d[a])
    return d


def halves(matrix):
    front, back = matrix[:4, :4], matrix[:4, ::-1][:, :4]
    return (front + back) / 2, (front - back) / 2


D_EVEN, D_ODD = halves(derivative_matrix())
T_EVEN, T_ODD = halves(derivative_matrix().T)
HATS = np.stack([(1.0 - node_points()) / 2, (1.0 + node_points()) / 2])


def mirrored(even, odd, u):
    total = [u[m] + u[7 - m] for m in range(4)]
    apart = [u[m] - u[7 - m] for m in range(4)]
    front, back = [], []
    for a in range(4):
        e = float(even[a, 0]) * total[0]
        o = float(odd[a, 0]) * apart[0]
        for m in range(1, 4):
            e = e + float(even[a, m]) * total[m]
            o = o + float(odd[a, m]) * apart[m]
        front.append(o + e)
        back.append(o - e)
    return front + back[::-1]


def split(x):
    high = x.astype(BF16)
    return high, (x - high.astype(F32)).astype(BF16)


def iota(shape, dim):
    return lax.broadcasted_iota(jnp.int32, shape, dim)


def kernel(
    n_x,
    n_y,
    res_hbm,
    diag_hbm,
    cross_hbm,
    fdm_hbm,
    eig_hbm,
    vid_hbm,
    inv_hbm,
    live_hbm,
    sface_hbm,
    scode_hbm,
    pface_hbm,
    pcode_hbm,
    direction_out,
    image_out,
    sums_out,
    live_ref,
    vid_ref,
    eig_ref,
    sface_ref,
    scode_ref,
    pface_ref,
    pcode_ref,
    rm,
    diag,
    cross,
    fdm,
    block,
    blocks,
    buf_a,
    buf_b,
    field,
    turned,
    turned2,
    grad1,
    direction,
    x_one,
    y_one,
    h_one,
    part,
    rc1,
    own2,
    rc2,
    own3,
    rc3,
    own4,
    rc4,
    coarse,
    idm,
    cdm,
    onehot,
    masks,
    perm,
    faces,
    out1,
    inc1,
    out2,
    inc2,
    picked,
    own_a,
    rc_a,
    own_b,
    rc_b,
    totals,
    ready,
    in_sem,
    out_sem,
    send_sem,
    recv_sem,
):
    x, y = lax.axis_index("gx"), lax.axis_index("gy")
    z, core = x // 2, lax.rem(x, 2)
    n_z, n_p = n_x // 2, 2 * n_y
    me = core * n_y + y
    offsets = (1, n_y - 1, 2, n_y - 2, n_y // 2)
    back_to = (1, 0, 3, 2, 4)

    moved = dict(
        live=(live_hbm, live_ref),
        residual=(res_hbm, rm),
        vid=(vid_hbm, vid_ref),
        sface=(sface_hbm, sface_ref),
        scode=(scode_hbm, scode_ref),
        pface=(pface_hbm, pface_ref),
        pcode=(pcode_hbm, pcode_ref),
        fdm=(fdm_hbm, fdm),
        eig=(eig_hbm, eig_ref),
        diag=(diag_hbm, diag),
        cross=(cross_hbm, cross),
    )
    loads = {n: pltpu.make_async_copy(s, d, in_sem.at[i]) for i, (n, (s, d)) in enumerate(moved.items())}
    for load in loads.values():
        load.start()

    barrier = pltpu.get_barrier_semaphore()

    def at_plane(k):
        k = k + k // 10
        a, b = y // 4 + 2 + k // 4, y + 2 + k
        return 4 * lax.rem(a, 4) + lax.rem(b, 4)

    def over_plane(act):
        def body(k, c):
            other = at_plane(k)
            for half in range(2):
                act(2 * z + half, other, half * n_y + other)
            return c

        lax.fori_loop(0, n_y - 1, body, 0)
        act(2 * z + 1 - core, y, (1 - core) * n_y + y)

    def over_line(act):
        def body(k, c):
            away = (k + 1) // 2
            act(lax.rem(z + n_z + n_z // 2 + away * (1 - 2 * lax.rem(k, 2)), n_z))
            return c

        lax.fori_loop(0, n_z - 1, body, 0)

    def at_device(i, j):
        return dict(device_id=(i, j), device_id_type=MESH)

    def greet_plane(k, c):
        pl.semaphore_signal(barrier, inc=1, **at_device(2 * z, at_plane(k)))
        return c

    lax.fori_loop(0, n_y - 1, greet_plane, 0)

    @pl.when(core == 1)
    def _():
        pl.semaphore_signal(barrier, inc=1, **at_device(2 * z, y))

    over_line(lambda t: pl.semaphore_signal(barrier, inc=1, **at_device(2 * t + 1, y)))

    sent = []

    def send(source, target, phase, i, j):
        pltpu.make_async_remote_copy(
            src_ref=source,
            dst_ref=target,
            send_sem=send_sem.at[phase],
            recv_sem=recv_sem.at[phase],
            **at_device(i, j),
        ).start()

    def send_plane(source, landing, phase):
        over_plane(lambda i, j, t: send(source(t), landing.at[me], phase, i, j))
        sent.append((phase, landing.at[pl.ds(0, n_p - 1)]))

    def send_line(source, landing, phase):
        over_line(lambda t: send(source, landing.at[z], phase, 2 * t + core, y))
        sent.append((phase, landing.at[pl.ds(0, n_z - 1)]))

    def await_all(phase, landing, n):
        some = landing.at[pl.ds(0, n - 1)]
        pltpu.make_async_copy(some, some, recv_sem.at[phase]).wait()

    loads["live"].wait()
    alive = (iota((1, LANES), 1) < live_ref[0]).astype(F32)
    lane = iota((1, LANES), 1)
    sub8 = iota((EDGE, 1), 0)
    hat_rows = []
    for c in range(2):
        h = jnp.zeros((EDGE, 1), F32)
        for k in range(EDGE):
            h = jnp.where(sub8 == k, float(HATS[c, k]), h)
        hat_rows.append(h)

    inc1[pl.ds(SPARE, 8), :] = jnp.zeros((8, LANES), F32)
    inc2[pl.ds(SPARE, 8), :] = jnp.zeros((8, LANES), F32)
    loads["residual"].wait()
    loads["vid"].wait()
    along_i = [None, None]
    for i in range(EDGE):
        slab = rm[pl.ds(64 * i, 64), :] * alive
        rm[pl.ds(64 * i, 64), :] = slab
        for c in range(2):
            term = float(HATS[c, i]) * slab
            along_i[c] = term if i == 0 else along_i[c] + term
    high_iota = iota((64, LANES), 0)
    low_iota = iota((LANES, LANES), 0)
    for ci in range(2):
        for cj in range(2):
            plane = float(HATS[cj, 0]) * along_i[ci][0:8]
            for j in range(1, EDGE):
                plane = plane + float(HATS[cj, j]) * along_i[ci][8 * j : 8 * j + 8]
            for ck in range(2):
                c = 4 * ci + 2 * cj + ck
                value = jnp.sum(plane * hat_rows[ck], axis=0, keepdims=True)
                ids = vid_ref[c : c + 1, :]
                at = pl.ds(c * LANES, LANES)
                here = (high_iota == (ids >> 7)).astype(F32)
                h_one[:, at] = here
                high, low = split(here * value)
                x_one[0:64, at] = high
                x_one[64:128, at] = low
                y_one[:, at] = (low_iota == (ids & 127)).astype(F32).astype(BF16)
    both = lax.dot_general(x_one[...], y_one[...], NT, preferred_element_type=F32)
    partial = both[0:64] + both[64:128]
    for q in range(n_p):
        part[q] = partial[2 * q : 2 * q + 2]

    @pl.when(core == 0)
    def _():
        pl.semaphore_wait(barrier, n_p - 1)
        pl.semaphore_signal(ready, inc=1, **at_device(2 * z + 1, y))

    @pl.when(core == 1)
    def _():
        pl.semaphore_wait(ready, 1)

    send_plane(lambda t: part.at[t], rc1, 0)
    rc1[me] = part[me]
    send_plane(lambda t: inv_hbm.at[:, pl.ds(pl.multiple_of(256 * t, 256), 256)], block, 9)
    keep = pltpu.make_async_copy(inv_hbm.at[:, pl.ds(pl.multiple_of(256 * me, 256), 256)], block.at[me], in_sem.at[12])
    keep.start()

    def column(row, rows, swap=0):
        width = row.shape[1]
        diagonal = (iota((rows, width), 0) ^ swap) == iota((rows, width), 1)
        kept = jnp.where(diagonal, row.astype(F32) + 1.0, 0.0)
        return jnp.broadcast_to(jnp.sum(kept, axis=1, keepdims=True) - 1.0, (rows, LANES))

    for name in ("sface", "scode", "pface", "pcode"):
        loads[name].wait()
    idm[pl.ds(0, 32), :] = column(sface_ref[0, pl.ds(y, 1), :], 32, 1)
    idm[pl.ds(32, 32), :] = column(sface_ref[0, pl.ds(y, 1), :], 32)
    cdm[pl.ds(0, 32), :] = column(scode_ref[0, pl.ds(y, 1), :], 32)
    for g in range(5):
        peer = lax.rem(y + offsets[g], n_y)
        at = PEER_ROW + PEER_ROWS * g
        idm[pl.ds(at, PEER_ROWS), :] = column(sface_ref[0, pl.ds(peer, 1), :], PEER_ROWS)
        cdm[pl.ds(at - FIRST, PEER_ROWS), :] = column(scode_ref[0, pl.ds(peer, 1), :], PEER_ROWS)
    idm[pl.ds(SPARE, 8), :] = jnp.full((8, LANES), -1.0, F32)
    cdm[pl.ds(SPARE - FIRST, 8), :] = jnp.full((8, LANES), -1.0, F32)
    for s in range(2):
        at = PIPE_ROW + PIPE_ROWS * s
        idm[pl.ds(at, PIPE_ROWS), :] = column(pface_ref[0, s : s + 1, :], PIPE_ROWS)
        cdm[pl.ds(at - FIRST, PIPE_ROWS), :] = column(pcode_ref[0, s : s + 1, :], PIPE_ROWS)
    ids = idm[...]
    for f in range(6):
        onehot[:, pl.ds(f * LANES, LANES)] = (ids == (6 * lane + f).astype(F32)).astype(F32).astype(BF16)
    codes = cdm[...]
    half = (lane >> 6).astype(F32)
    for p in range(4):
        masks[:, pl.ds(p * LANES, LANES)] = (codes == 2.0 * p + half).astype(F32).astype(BF16)
    grid_row = iota((LANES, LANES), 0)
    grid_lane = iota((LANES, LANES), 1)
    first, second = (grid_row & 63) >> 3, grid_row & 7
    flip = 7 * (grid_lane >> 6)
    for t in range(8):
        a, b = (second, first) if t % 4 >= 2 else (first, second)
        b = b ^ 7 if t % 2 == 1 else b
        source = 8 * (a ^ flip) + b
        fits = (source == (grid_lane & 63)) & ((grid_row < 64) if t < 4 else (grid_row >= 64))
        perm[:, pl.ds(t * LANES, LANES)] = fits.astype(F32).astype(BF16)

    await_all(0, rc1, n_p)
    mine = jnp.sum(rc1[...], axis=0)
    own2[...] = mine
    rc2[z] = mine

    @pl.when(core == 1)
    def _():
        pl.semaphore_wait(barrier, 2 * (n_z - 1))
        pl.semaphore_signal(ready, inc=1, **at_device(2 * z, y))

    @pl.when(core == 0)
    def _():
        pl.semaphore_wait(ready, 1)

    send_line(own2, rc2, 1)

    def sum_of(coef, slabs, a):
        total = coef(0, a) * slabs(0)
        for m in range(1, EDGE):
            total = total + coef(m, a) * slabs(m)
        return total

    def per_row(body):
        def step(a, c):
            body(a)
            return c

        lax.fori_loop(0, EDGE, step, 0)

    def slab_i(ref):
        return lambda m: ref[pl.ds(pl.multiple_of(64 * m, 64), 64), :]

    def slab_j(ref):
        cube = ref.reshape(EDGE, EDGE, EDGE, LANES)
        return lambda m: cube[:, m].reshape(64, LANES)

    def forward(d):
        return lambda m, a: fdm[d, m, pl.ds(a, 1), :]

    def backward(d):
        return lambda m, a: fdm[d, a, m : m + 1, :]

    def put_i(ref, a, value):
        ref[pl.ds(pl.multiple_of(64 * a, 64), 64), :] = value

    def put_j(ref, a, value):
        ref.reshape(EDGE, EDGE, EDGE, LANES)[:, pl.ds(a, 1)] = value.reshape(EDGE, 1, EDGE, LANES)

    loads["fdm"].wait()
    loads["eig"].wait()
    per_row(lambda a: put_i(buf_a, a, sum_of(forward(0), slab_i(rm), a)))
    per_row(lambda a: put_j(buf_b, a, sum_of(forward(1), slab_j(buf_a), a)))
    for k in range(EDGE):
        turned[pl.ds(64 * k, 64), :] = buf_b[pl.ds(k, 64, stride=EDGE), :]
    base = jnp.concatenate([eig_ref[0, a : a + 1, :] + eig_ref[1] for a in range(EDGE)], axis=0)
    buf_a[pl.ds(0, 64), :] = base

    def spectral(a):
        value = sum_of(forward(2), slab_i(turned), a)
        put_i(buf_b, a, value / (buf_a[pl.ds(0, 64), :] + eig_ref[2, pl.ds(a, 1), :]))

    per_row(spectral)

    per_row(lambda a: put_i(turned, a, sum_of(backward(2), slab_i(buf_b), a)))
    for k in range(EDGE):
        buf_a[pl.ds(k, 64, stride=EDGE), :] = turned[pl.ds(64 * k, 64), :]
    per_row(lambda a: put_j(buf_b, a, sum_of(backward(1), slab_j(buf_a), a)))
    per_row(lambda a: put_i(field, a, sum_of(backward(0), slab_i(buf_b), a)))

    def face_of(ref, f):
        if f < 2:
            return ref[pl.ds(448 * f, 64), :]
        if f < 4:
            return slab_j(ref)(7 * (f - 2))
        return ref[pl.ds(7 * (f - 4), 64, stride=EDGE), :]

    def send_faces(ref, out, inc, phase):
        for f in range(6):
            high, low = split(face_of(ref, f))
            faces[0:64, pl.ds(f * LANES, LANES)] = high
            faces[64:128, pl.ds(f * LANES, LANES)] = low
        found = lax.dot_general(onehot[...], faces[...], NT, preferred_element_type=F32)
        found = found + pltpu.roll(found, 64, 1)
        out[...] = found
        inc[pl.ds(FIRST, 32), :] = found[0:32]
        hops = [
            (PEER_ROW + PEER_ROWS * g, PEER_ROW + PEER_ROWS * back_to[g], PEER_ROWS, (x, lax.rem(y + offsets[g], n_y)))
            for g in range(5)
        ] + [
            (
                PIPE_ROW + PIPE_ROWS * s,
                PIPE_ROW + PIPE_ROWS * (1 - s),
                PIPE_ROWS,
                (lax.rem(x + n_x - 1 + 2 * s, n_x), y),
            )
            for s in range(2)
        ]
        for start, land, count, target in hops:
            send(out.at[pl.ds(start, count)], inc.at[pl.ds(land, count)], phase, *target)
        sent.append((phase, inc.at[pl.ds(0, SENT_ROWS)]))

    def await_faces(phase, inc):
        some = inc.at[pl.ds(0, SENT_ROWS)]
        pltpu.make_async_copy(some, some, recv_sem.at[phase]).wait()

    def place_faces(ref, inc):
        high, low = split(inc[pl.ds(FIRST, USED), :])
        for p in range(4):
            mask = masks[:, pl.ds(p * LANES, LANES)]
            picked[:, pl.ds(p * LANES, LANES)] = high * mask
            picked[:, pl.ds((p + 4) * LANES, LANES)] = low * mask
        across = lax.dot_general(perm[...], picked[...], NT, preferred_element_type=F32)
        extra = jnp.dot(across.astype(BF16), onehot[pl.ds(FIRST, USED), :], preferred_element_type=F32)
        extra = extra[0:64] + extra[64:128]
        cube = ref.reshape(EDGE, EDGE, EDGE, LANES)
        for f in range(6):
            more = extra[:, f * LANES : (f + 1) * LANES]
            if f < 2:
                ref[pl.ds(448 * f, 64), :] += more
            elif f < 4:
                cube[:, 7 * (f - 2)] += more.reshape(EDGE, EDGE, LANES)
            else:
                at = pl.ds(7 * (f - 4), 64, stride=EDGE)
                ref[at, :] = ref[at, :] + more

    await_all(9, block, n_p)
    keep.wait()
    for n in range(n_p):
        high, low = split(block[n])
        blocks[16 * n : 16 * n + 16, :] = high
        blocks[16 * (n_p + n) : 16 * (n_p + n) + 16, :] = low

    await_all(1, rc2, n_z)
    mine = jnp.sum(rc2[...], axis=0)
    high, low = split(jnp.concatenate([mine[0:1], mine[1:2]], axis=1))
    pair = jnp.concatenate([high.astype(F32), low.astype(F32), jnp.zeros((14, 2 * LANES), F32)], axis=0).astype(BF16)
    product = lax.dot_general(pair, blocks[...], NT, preferred_element_type=F32)
    count = 16 * n_p
    product = product[0:1, :count] + (product[1:2, :count] + product[0:1, count:])
    mine = jnp.concatenate([product[:, LANES * h : LANES * h + LANES] for h in range(4)], axis=0)
    own3[...] = mine
    rc3[me] = mine
    send_plane(lambda t: own3, rc3, 2)

    send_faces(field, out1, inc1, 7)

    await_all(2, rc3, n_p)
    mine = jnp.sum(rc3[...], axis=0)
    own4[...] = mine
    rc4[z] = mine
    send_line(own4, rc4, 3)
    await_faces(7, inc1)
    place_faces(field, inc1)
    loads["diag"].wait()
    loads["cross"].wait()

    await_all(3, rc4, n_z)
    for q in range(n_z):
        coarse[pl.ds(4 * q, 4), :] = rc4[q]

    high, low = split(coarse[...])
    at_low = jnp.dot(jnp.concatenate([high, low], axis=0), y_one[...], preferred_element_type=F32)
    corner = jnp.sum((at_low[0:64] + at_low[64:128]) * h_one[...], axis=0, keepdims=True)
    planes = []
    for ci in range(2):
        lines = []
        for cj in range(2):
            at = (4 * ci + 2 * cj) * LANES
            lines.append(hat_rows[0] * corner[:, at : at + LANES] + hat_rows[1] * corner[:, at + LANES : at + 2 * LANES])
        planes.append(
            jnp.concatenate(
                [float(HATS[0, j]) * lines[0] + float(HATS[1, j]) * lines[1] for j in range(EDGE)], axis=0
            )
        )
    for i in range(EDGE):
        at = pl.ds(64 * i, 64)
        lifted = float(HATS[0, i]) * planes[0] + float(HATS[1, i]) * planes[1]
        direction[at, :] = alive * (field[at, :] + lifted)

    stores = [pltpu.make_async_copy(direction, direction_out, out_sem.at[0])]
    stores[0].start()

    def take(ref, start, stride):
        return [ref[pl.ds(pl.multiple_of(start + stride * m, 8), 8), :] for m in range(EDGE)]

    def along_first(j, c):
        result = mirrored(D_EVEN, D_ODD, take(direction, 8 * j, 64))
        for a in range(EDGE):
            grad1[pl.ds(pl.multiple_of(64 * a + 8 * j, 8), 8), :] = result[a]
        return c

    lax.fori_loop(0, EDGE, along_first, 0)

    def turn(values, ref):
        for m in range(EDGE):
            ref[pl.ds(EDGE * m, EDGE), :] = values[m]
        return [ref[pl.ds(m, EDGE, stride=EDGE), :] for m in range(EDGE)]

    def middle(i, sums):
        curve, dots = sums
        start = pl.multiple_of(64 * i, 64)
        slab = pl.ds(start, 64)
        d = take(direction, start, 8)
        across = turn(d, turned.at[pl.ds(0, 64)])
        g3 = turn(mirrored(D_EVEN, D_ODD, across), turned.at[pl.ds(64, 64)])
        g2 = mirrored(D_EVEN, D_ODD, d)
        g1 = take(grad1, start, 8)
        m = [diag[q, slab, :].astype(F32) for q in range(3)] + [cross[q, slab, :].astype(F32) for q in range(3)]
        f2, f3 = [], []
        for j in range(EDGE):
            rr, ss, tt, rs, rt, st = [q[8 * j : 8 * j + 8] for q in m]
            u = rr * g1[j] + rs * g2[j] + rt * g3[j]
            v = rs * g1[j] + ss * g2[j] + st * g3[j]
            w = rt * g1[j] + st * g2[j] + tt * g3[j]
            curve = curve + (g1[j] * u + g2[j] * v) + (g3[j] * w + d[j] * d[j])
            grad1[pl.ds(start + 8 * j, 8), :] = u
            f2.append(v)
            f3.append(w)
        dots = dots + jnp.sum((rm[slab, :] * direction[slab, :]).reshape(EDGE, EDGE, LANES), axis=0)
        b3 = turn(mirrored(T_EVEN, T_ODD, turn(f3, turned2.at[pl.ds(0, 64)])), turned2.at[pl.ds(64, 64)])
        b2 = mirrored(T_EVEN, T_ODD, f2)
        for j in range(EDGE):
            field[pl.ds(start + 8 * j, 8), :] = (b2[j] + b3[j]) + d[j]
        return curve, dots

    zero = jnp.zeros((EDGE, LANES), F32)
    curve, dots = lax.fori_loop(0, EDGE, middle, (zero, zero))

    def back_first(j, c):
        result = mirrored(T_EVEN, T_ODD, take(grad1, 8 * j, 64))
        for a in range(EDGE):
            at = pl.ds(pl.multiple_of(64 * a + 8 * j, 8), 8)
            field[at, :] = field[at, :] + result[a]
        return c

    lax.fori_loop(0, EDGE, back_first, 0)

    send_faces(field, out2, inc2, 8)

    def folded(a, b):
        return jnp.sum((a * b).reshape(POINTS // EDGE, EDGE, LANES), axis=0)

    old = folded(rm[...], rm[...])
    await_faces(8, inc2)
    place_faces(field, inc2)

    stores.append(pltpu.make_async_copy(field, image_out, out_sem.at[1]))
    stores[1].start()
    image = field[...]
    mixed = folded(rm[...], image)
    square = folded(image, image)
    sums = jnp.zeros((1, LANES), F32)
    for q, value in enumerate((dots, curve, old, mixed, square)):
        one = jnp.sum(jnp.sum(value, axis=0, keepdims=True), axis=1, keepdims=True)
        sums = jnp.where(lane == q, one, sums)
    own_a[...] = sums
    rc_a[me] = sums
    send_plane(lambda t: own_a, rc_a, 5)
    await_all(5, rc_a, n_p)
    sums = jnp.sum(rc_a[...], axis=0)
    own_b[...] = sums
    rc_b[z] = sums
    send_line(own_b, rc_b, 6)
    await_all(6, rc_b, n_z)
    sums = jnp.sum(rc_b[...], axis=0)

    totals[...] = sums
    stores.append(pltpu.make_async_copy(totals, sums_out, out_sem.at[2]))
    stores[2].start()
    for phase, some in sent:
        pltpu.make_async_copy(some, some, send_sem.at[phase]).wait()
    for store in stores:
        store.wait()


def update(
    sol_hbm,
    res_hbm,
    direction_hbm,
    image_hbm,
    sums_hbm,
    live_hbm,
    sol_out,
    res_out,
    ratio_out,
    sol,
    res,
    direction,
    image,
    sums_ref,
    live_ref,
    in_sem,
    small_sem,
    out_sem,
):
    small = [
        pltpu.make_async_copy(s, d, small_sem.at[i]) for i, (s, d) in enumerate(((sums_hbm, sums_ref), (live_hbm, live_ref)))
    ]
    for copy in small:
        copy.start()
    half = POINTS // 2
    loads = []
    for h in range(2):
        at = pl.ds(half * h, half)
        for q, (s, d) in enumerate(((sol_hbm, sol), (direction_hbm, direction), (res_hbm, res), (image_hbm, image))):
            loads.append(pltpu.make_async_copy(s.at[at], d.at[at], in_sem.at[h, q]))
    for copy in loads:
        copy.start()
    for copy in small:
        copy.wait()
    lane = iota((1, LANES), 1)
    sums = sums_ref[...]

    def total(q):
        return jnp.sum(jnp.where(lane == q, sums, 0.0), axis=1, keepdims=True)

    step = total(0) / total(1)
    alive = (lane < live_ref[0]).astype(F32)
    stores = []
    for h in range(2):
        at = pl.ds(half * h, half)
        for copy in loads[4 * h : 4 * h + 4]:
            copy.wait()
        sol[at, :] = alive * (sol[at, :] + step * direction[at, :])
        res[at, :] = res[at, :] * alive - step * image[at, :]
        for q, (s, d) in enumerate(((sol, sol_out), (res, res_out))):
            store = pltpu.make_async_copy(s.at[at], d.at[at], out_sem.at[h, q])
            store.start()
            stores.append(store)
    ratio = (total(2) - 2.0 * step * total(3) + step * step * total(4)) / total(2)
    ratio_out[0] = jnp.sum(ratio)
    for store in stores:
        store.wait()


def on_device(n_x, n_y, *args):
    live, vid, eig, sface, scode, pface, pcode = (args[i] for i in (8, 6, 5, 9, 10, 11, 12))
    smem = pl.BlockSpec(memory_space=pltpu.SMEM)
    hbm = pl.BlockSpec(memory_space=pl.ANY)
    n_p, n_z = 2 * n_y, n_x // 2
    field = pltpu.VMEM((POINTS, LANES), F32)
    whole = jax.ShapeDtypeStruct((POINTS, LANES), F32)
    direction, image, sums = pl.pallas_call(
        functools.partial(kernel, n_x, n_y),
        out_shape=(whole, whole, jax.ShapeDtypeStruct((1, LANES), F32)),
        in_specs=[hbm] * 12,
        out_specs=(hbm, hbm, hbm),
        scratch_shapes=[
            pltpu.SMEM((1,), jnp.int32),
            pltpu.VMEM(vid.shape, jnp.int32),
            pltpu.VMEM(eig.shape, F32),
            pltpu.VMEM(sface.shape, jnp.int32),
            pltpu.VMEM(scode.shape, jnp.int32),
            pltpu.VMEM(pface.shape, jnp.int32),
            pltpu.VMEM(pcode.shape, jnp.int32),
            field,
            pltpu.VMEM((3, POINTS, LANES), BF16),
            pltpu.VMEM((3, POINTS, LANES), BF16),
            pltpu.VMEM((3, EDGE, EDGE, LANES), F32),
            pltpu.VMEM((n_p, 16, 2 * LANES), F32),
            pltpu.VMEM((32 * n_p, 2 * LANES), BF16),
            field,
            field,
            field,
            field,
            field,
            field,
            field,
            pltpu.VMEM((LANES, 8 * LANES), BF16),
            pltpu.VMEM((LANES, 8 * LANES), BF16),
            pltpu.VMEM((64, 8 * LANES), F32),
            pltpu.VMEM((n_p, 2, LANES), F32),
            pltpu.VMEM((n_p, 2, LANES), F32),
            pltpu.VMEM((2, LANES), F32),
            pltpu.VMEM((n_z, 2, LANES), F32),
            pltpu.VMEM((4, LANES), F32),
            pltpu.VMEM((n_p, 4, LANES), F32),
            pltpu.VMEM((4, LANES), F32),
            pltpu.VMEM((n_z, 4, LANES), F32),
            pltpu.VMEM((64, LANES), F32),
            pltpu.VMEM((ROWS, LANES), F32),
            pltpu.VMEM((USED, LANES), F32),
            pltpu.VMEM((ROWS, 6 * LANES), BF16),
            pltpu.VMEM((USED, 4 * LANES), BF16),
            pltpu.VMEM((LANES, 8 * LANES), BF16),
            pltpu.VMEM((LANES, 6 * LANES), BF16),
            pltpu.VMEM((ROWS, LANES), F32),
            pltpu.VMEM((ROWS, LANES), F32),
            pltpu.VMEM((ROWS, LANES), F32),
            pltpu.VMEM((ROWS, LANES), F32),
            pltpu.VMEM((USED, 8 * LANES), BF16),
            pltpu.VMEM((1, LANES), F32),
            pltpu.VMEM((n_p, 1, LANES), F32),
            pltpu.VMEM((1, LANES), F32),
            pltpu.VMEM((n_z, 1, LANES), F32),
            pltpu.VMEM((1, LANES), F32),
            pltpu.SemaphoreType.REGULAR,
            pltpu.SemaphoreType.DMA((13,)),
            pltpu.SemaphoreType.DMA((3,)),
            pltpu.SemaphoreType.DMA((10,)),
            pltpu.SemaphoreType.DMA((10,)),
        ],
        compiler_params=pltpu.CompilerParams(
            collective_id=0, has_side_effects=True, vmem_limit_bytes=60 * 1024 * 1024
        ),
    )(*args[1:])
    return pl.pallas_call(
        update,
        out_shape=(whole, whole, jax.ShapeDtypeStruct((1,), F32)),
        in_specs=[hbm] * 6,
        out_specs=(hbm, hbm, smem),
        scratch_shapes=[
            field,
            field,
            field,
            field,
            pltpu.VMEM((1, LANES), F32),
            pltpu.SMEM((1,), jnp.int32),
            pltpu.SemaphoreType.DMA((2, 4)),
            pltpu.SemaphoreType.DMA((2,)),
            pltpu.SemaphoreType.DMA((2, 2)),
        ],
        compiler_params=pltpu.CompilerParams(vmem_limit_bytes=60 * 1024 * 1024),
    )(args[0], args[1], direction, image, sums, live)


def solution(mesh):
    both = ("gx", "gy")
    placed = (
        P(None, both),
        P(None, both),
        P(None, None, both),
        P(None, None, both),
        P(None, None, None, both),
        P(None, None, both),
        P(None, both),
        P(both, None),
        P(both),
        P(both, None, None),
        P(both, None, None),
        P(both, None, None),
        P(both, None, None),
    )
    return jax.shard_map(
        functools.partial(on_device, mesh.shape["gx"], mesh.shape["gy"]),
        mesh=mesh,
        in_specs=placed,
        out_specs=(P(None, both), P(None, both), P()),
        check_vma=False,
    )
```

```python
import functools

import numpy as np
import jax
import jax.numpy as jnp
from jax import lax
from jax.experimental import pallas as pl
from jax.experimental.pallas import tpu as pltpu
from jax.sharding import PartitionSpec as P

EDGE = 8
LANES = 128
POINTS = 512
F32 = jnp.float32
BF16 = jnp.bfloat16
MESH = pl.DeviceIdType.MESH
NT = (((1,), (1,)), ((), ()))

ROWS = 320
FIRST = 32
PEER_ROW = 64
PEER_ROWS = 24
SPARE = 184
PIPE_ROW = 192
PIPE_ROWS = 64
SENT_ROWS = 5 * PEER_ROWS + 2 * PIPE_ROWS
USED = ROWS - FIRST


def node_points():
    return -np.cos(np.pi * np.arange(EDGE) / (EDGE - 1))


def derivative_matrix():
    t = node_points()
    c = np.where((np.arange(EDGE) == 0) | (np.arange(EDGE) == EDGE - 1), 2.0, 1.0)
    d = np.zeros((EDGE, EDGE))
    for a in range(EDGE):
        for b in range(EDGE):
            if a != b:
                d[a, b] = c[a] / c[b] * (-1.0) ** (a + b) / (t[a] - t[b])
    for a in range(EDGE):
        d[a, a] = -np.sum(d[a])
    return d


def halves(matrix):
    front, back = matrix[:4, :4], matrix[:4, ::-1][:, :4]
    return (front + back) / 2, (front - back) / 2


D_EVEN, D_ODD = halves(derivative_matrix())
T_EVEN, T_ODD = halves(derivative_matrix().T)
HATS = np.stack([(1.0 - node_points()) / 2, (1.0 + node_points()) / 2])


def mirrored(even, odd, u):
    total = [u[m] + u[7 - m] for m in range(4)]
    apart = [u[m] - u[7 - m] for m in range(4)]
    front, back = [], []
    for a in range(4):
        e = float(even[a, 0]) * total[0]
        o = float(odd[a, 0]) * apart[0]
        for m in range(1, 4):
            e = e + float(even[a, m]) * total[m]
            o = o + float(odd[a, m]) * apart[m]
        front.append(o + e)
        back.append(o - e)
    return front + back[::-1]


def split(x):
    high = x.astype(BF16)
    return high, (x - high.astype(F32)).astype(BF16)


def iota(shape, dim):
    return lax.broadcasted_iota(jnp.int32, shape, dim)


def kernel(
    n_x,
    n_y,
    sol_hbm,
    res_hbm,
    diag_hbm,
    cross_hbm,
    fdm_hbm,
    eig_hbm,
    vid_hbm,
    inv_hbm,
    live_hbm,
    sface_hbm,
    scode_hbm,
    pface_hbm,
    pcode_hbm,
    sol,
    rm,
    direction,
    field,
    totals,
    live_ref,
    vid_ref,
    eig_ref,
    sface_ref,
    scode_ref,
    pface_ref,
    pcode_ref,
    diag,
    cross,
    fdm,
    block,
    blocks,
    buf_a,
    buf_b,
    turned,
    turned2,
    grad1,
    x_one,
    y_one,
    h_one,
    part,
    rc1,
    own2,
    rc2,
    own3,
    rc3,
    own4,
    rc4,
    coarse,
    idm,
    cdm,
    onehot,
    masks,
    perm,
    faces,
    out1,
    inc1,
    out2,
    inc2,
    picked,
    own_a,
    rc_a,
    own_b,
    rc_b,
    ready,
    in_sem,
    send_sem,
    recv_sem,
):
    x, y = lax.axis_index("gx"), lax.axis_index("gy")
    z, core = x // 2, lax.rem(x, 2)
    n_z, n_p = n_x // 2, 2 * n_y
    me = core * n_y + y
    offsets = (1, n_y - 1, 2, n_y - 2, n_y // 2)
    back_to = (1, 0, 3, 2, 4)

    moved = dict(
        live=(live_hbm, live_ref),
        residual=(res_hbm, rm),
        vid=(vid_hbm, vid_ref),
        sface=(sface_hbm, sface_ref),
        scode=(scode_hbm, scode_ref),
        pface=(pface_hbm, pface_ref),
        pcode=(pcode_hbm, pcode_ref),
        fdm=(fdm_hbm, fdm),
        eig=(eig_hbm, eig_ref),
        diag=(diag_hbm, diag),
        cross=(cross_hbm, cross),
        sol=(sol_hbm, sol),
    )
    loads = {n: pltpu.make_async_copy(s, d, in_sem.at[i]) for i, (n, (s, d)) in enumerate(moved.items())}
    for load in loads.values():
        load.start()

    barrier = pltpu.get_barrier_semaphore()

    def at_plane(k):
        k = k + k // 10
        a, b = y // 4 + 2 + k // 4, y + 2 + k
        return 4 * lax.rem(a, 4) + lax.rem(b, 4)

    def over_plane(act):
        def body(k, c):
            other = at_plane(k)
            for half in range(2):
                act(2 * z + half, other, half * n_y + other)
            return c

        lax.fori_loop(0, n_y - 1, body, 0)
        act(2 * z + 1 - core, y, (1 - core) * n_y + y)

    def over_line(act):
        def body(k, c):
            away = (k + 1) // 2
            act(lax.rem(z + n_z + n_z // 2 + away * (1 - 2 * lax.rem(k, 2)), n_z))
            return c

        lax.fori_loop(0, n_z - 1, body, 0)

    def at_device(i, j):
        return dict(device_id=(i, j), device_id_type=MESH)

    def greet_plane(k, c):
        pl.semaphore_signal(barrier, inc=1, **at_device(2 * z, at_plane(k)))
        return c

    lax.fori_loop(0, n_y - 1, greet_plane, 0)

    @pl.when(core == 1)
    def _():
        pl.semaphore_signal(barrier, inc=1, **at_device(2 * z, y))

    over_line(lambda t: pl.semaphore_signal(barrier, inc=1, **at_device(2 * t + 1, y)))

    sent = []

    def send(source, target, phase, i, j):
        pltpu.make_async_remote_copy(
            src_ref=source,
            dst_ref=target,
            send_sem=send_sem.at[phase],
            recv_sem=recv_sem.at[phase],
            **at_device(i, j),
        ).start()

    def send_plane(source, landing, phase):
        over_plane(lambda i, j, t: send(source(t), landing.at[me], phase, i, j))
        sent.append((phase, landing.at[pl.ds(0, n_p - 1)]))

    def send_line(source, landing, phase):
        over_line(lambda t: send(source, landing.at[z], phase, 2 * t + core, y))
        sent.append((phase, landing.at[pl.ds(0, n_z - 1)]))

    def await_all(phase, landing, n):
        some = landing.at[pl.ds(0, n - 1)]
        pltpu.make_async_copy(some, some, recv_sem.at[phase]).wait()

    loads["live"].wait()
    alive = (iota((1, LANES), 1) < live_ref[0]).astype(F32)
    lane = iota((1, LANES), 1)
    sub8 = iota((EDGE, 1), 0)
    hat_rows = []
    for c in range(2):
        h = jnp.zeros((EDGE, 1), F32)
        for k in range(EDGE):
            h = jnp.where(sub8 == k, float(HATS[c, k]), h)
        hat_rows.append(h)

    inc1[pl.ds(SPARE, 8), :] = jnp.zeros((8, LANES), F32)
    inc2[pl.ds(SPARE, 8), :] = jnp.zeros((8, LANES), F32)
    loads["residual"].wait()
    loads["vid"].wait()
    along_i = [None, None]
    for i in range(EDGE):
        slab = rm[pl.ds(64 * i, 64), :] * alive
        rm[pl.ds(64 * i, 64), :] = slab
        for c in range(2):
            term = float(HATS[c, i]) * slab
            along_i[c] = term if i == 0 else along_i[c] + term
    high_iota = iota((64, LANES), 0)
    low_iota = iota((LANES, LANES), 0)
    for ci in range(2):
        for cj in range(2):
            plane = float(HATS[cj, 0]) * along_i[ci][0:8]
            for j in range(1, EDGE):
                plane = plane + float(HATS[cj, j]) * along_i[ci][8 * j : 8 * j + 8]
            for ck in range(2):
                c = 4 * ci + 2 * cj + ck
                value = jnp.sum(plane * hat_rows[ck], axis=0, keepdims=True)
                ids = vid_ref[c : c + 1, :]
                at = pl.ds(c * LANES, LANES)
                here = (high_iota == (ids >> 7)).astype(F32)
                h_one[:, at] = here
                high, low = split(here * value)
                x_one[0:64, at] = high
                x_one[64:128, at] = low
                y_one[:, at] = (low_iota == (ids & 127)).astype(F32).astype(BF16)
    both = lax.dot_general(x_one[...], y_one[...], NT, preferred_element_type=F32)
    partial = both[0:64] + both[64:128]
    for q in range(n_p):
        part[q] = partial[2 * q : 2 * q + 2]

    @pl.when(core == 0)
    def _():
        pl.semaphore_wait(barrier, n_p - 1)
        pl.semaphore_signal(ready, inc=1, **at_device(2 * z + 1, y))

    @pl.when(core == 1)
    def _():
        pl.semaphore_wait(ready, 1)

    send_plane(lambda t: part.at[t], rc1, 0)
    rc1[me] = part[me]
    send_plane(lambda t: inv_hbm.at[:, pl.ds(pl.multiple_of(256 * t, 256), 256)], block, 9)
    keep = pltpu.make_async_copy(inv_hbm.at[:, pl.ds(pl.multiple_of(256 * me, 256), 256)], block.at[me], in_sem.at[13])
    keep.start()

    def column(row, rows, swap=0):
        width = row.shape[1]
        diagonal = (iota((rows, width), 0) ^ swap) == iota((rows, width), 1)
        kept = jnp.where(diagonal, row.astype(F32) + 1.0, 0.0)
        return jnp.broadcast_to(jnp.sum(kept, axis=1, keepdims=True) - 1.0, (rows, LANES))

    for name in ("sface", "scode", "pface", "pcode"):
        loads[name].wait()
    idm[pl.ds(0, 32), :] = column(sface_ref[0, pl.ds(y, 1), :], 32, 1)
    idm[pl.ds(32, 32), :] = column(sface_ref[0, pl.ds(y, 1), :], 32)
    cdm[pl.ds(0, 32), :] = column(scode_ref[0, pl.ds(y, 1), :], 32)
    for g in range(5):
        peer = lax.rem(y + offsets[g], n_y)
        at = PEER_ROW + PEER_ROWS * g
        idm[pl.ds(at, PEER_ROWS), :] = column(sface_ref[0, pl.ds(peer, 1), :], PEER_ROWS)
        cdm[pl.ds(at - FIRST, PEER_ROWS), :] = column(scode_ref[0, pl.ds(peer, 1), :], PEER_ROWS)
    idm[pl.ds(SPARE, 8), :] = jnp.full((8, LANES), -1.0, F32)
    cdm[pl.ds(SPARE - FIRST, 8), :] = jnp.full((8, LANES), -1.0, F32)
    for s in range(2):
        at = PIPE_ROW + PIPE_ROWS * s
        idm[pl.ds(at, PIPE_ROWS), :] = column(pface_ref[0, s : s + 1, :], PIPE_ROWS)
        cdm[pl.ds(at - FIRST, PIPE_ROWS), :] = column(pcode_ref[0, s : s + 1, :], PIPE_ROWS)
    ids = idm[...]
    for f in range(6):
        onehot[:, pl.ds(f * LANES, LANES)] = (ids == (6 * lane + f).astype(F32)).astype(F32).astype(BF16)
    codes = cdm[...]
    half = (lane >> 6).astype(F32)
    for p in range(4):
        masks[:, pl.ds(p * LANES, LANES)] = (codes == 2.0 * p + half).astype(F32).astype(BF16)
    grid_row = iota((LANES, LANES), 0)
    grid_lane = iota((LANES, LANES), 1)
    first, second = (grid_row & 63) >> 3, grid_row & 7
    flip = 7 * (grid_lane >> 6)
    for t in range(8):
        a, b = (second, first) if t % 4 >= 2 else (first, second)
        b = b ^ 7 if t % 2 == 1 else b
        source = 8 * (a ^ flip) + b
        fits = (source == (grid_lane & 63)) & ((grid_row < 64) if t < 4 else (grid_row >= 64))
        perm[:, pl.ds(t * LANES, LANES)] = fits.astype(F32).astype(BF16)

    await_all(0, rc1, n_p)
    mine = jnp.sum(rc1[...], axis=0)
    own2[...] = mine
    rc2[z] = mine

    @pl.when(core == 1)
    def _():
        pl.semaphore_wait(barrier, 2 * (n_z - 1))
        pl.semaphore_signal(ready, inc=1, **at_device(2 * z, y))

    @pl.when(core == 0)
    def _():
        pl.semaphore_wait(ready, 1)

    send_line(own2, rc2, 1)

    def sum_of(coef, slabs, a):
        total = coef(0, a) * slabs(0)
        for m in range(1, EDGE):
            total = total + coef(m, a) * slabs(m)
        return total

    def per_row(body):
        def step(a, c):
            body(a)
            return c

        lax.fori_loop(0, EDGE, step, 0)

    def slab_i(ref):
        return lambda m: ref[pl.ds(pl.multiple_of(64 * m, 64), 64), :]

    def slab_j(ref):
        cube = ref.reshape(EDGE, EDGE, EDGE, LANES)
        return lambda m: cube[:, m].reshape(64, LANES)

    def forward(d):
        return lambda m, a: fdm[d, m, pl.ds(a, 1), :]

    def backward(d):
        return lambda m, a: fdm[d, a, m : m + 1, :]

    def put_i(ref, a, value):
        ref[pl.ds(pl.multiple_of(64 * a, 64), 64), :] = value

    def put_j(ref, a, value):
        ref.reshape(EDGE, EDGE, EDGE, LANES)[:, pl.ds(a, 1)] = value.reshape(EDGE, 1, EDGE, LANES)

    loads["fdm"].wait()
    loads["eig"].wait()
    per_row(lambda a: put_i(buf_a, a, sum_of(forward(0), slab_i(rm), a)))
    per_row(lambda a: put_j(buf_b, a, sum_of(forward(1), slab_j(buf_a), a)))
    for k in range(EDGE):
        turned[pl.ds(64 * k, 64), :] = buf_b[pl.ds(k, 64, stride=EDGE), :]
    base = jnp.concatenate([eig_ref[0, a : a + 1, :] + eig_ref[1] for a in range(EDGE)], axis=0)
    buf_a[pl.ds(0, 64), :] = base

    def spectral(a):
        value = sum_of(forward(2), slab_i(turned), a)
        put_i(buf_b, a, value / (buf_a[pl.ds(0, 64), :] + eig_ref[2, pl.ds(a, 1), :]))

    per_row(spectral)

    per_row(lambda a: put_i(turned, a, sum_of(backward(2), slab_i(buf_b), a)))
    for k in range(EDGE):
        buf_a[pl.ds(k, 64, stride=EDGE), :] = turned[pl.ds(64 * k, 64), :]
    per_row(lambda a: put_j(buf_b, a, sum_of(backward(1), slab_j(buf_a), a)))
    per_row(lambda a: put_i(field, a, sum_of(backward(0), slab_i(buf_b), a)))

    def face_of(ref, f):
        if f < 2:
            return ref[pl.ds(448 * f, 64), :]
        if f < 4:
            return slab_j(ref)(7 * (f - 2))
        return ref[pl.ds(7 * (f - 4), 64, stride=EDGE), :]

    def send_faces(ref, out, inc, phase):
        for f in range(6):
            high, low = split(face_of(ref, f))
            faces[0:64, pl.ds(f * LANES, LANES)] = high
            faces[64:128, pl.ds(f * LANES, LANES)] = low
        found = lax.dot_general(onehot[...], faces[...], NT, preferred_element_type=F32)
        found = found + pltpu.roll(found, 64, 1)
        out[...] = found
        inc[pl.ds(FIRST, 32), :] = found[0:32]
        hops = [
            (PEER_ROW + PEER_ROWS * g, PEER_ROW + PEER_ROWS * back_to[g], PEER_ROWS, (x, lax.rem(y + offsets[g], n_y)))
            for g in range(5)
        ] + [
            (
                PIPE_ROW + PIPE_ROWS * s,
                PIPE_ROW + PIPE_ROWS * (1 - s),
                PIPE_ROWS,
                (lax.rem(x + n_x - 1 + 2 * s, n_x), y),
            )
            for s in range(2)
        ]
        for start, land, count, target in hops:
            send(out.at[pl.ds(start, count)], inc.at[pl.ds(land, count)], phase, *target)
        sent.append((phase, inc.at[pl.ds(0, SENT_ROWS)]))

    def await_faces(phase, inc):
        some = inc.at[pl.ds(0, SENT_ROWS)]
        pltpu.make_async_copy(some, some, recv_sem.at[phase]).wait()

    def place_faces(ref, inc):
        high, low = split(inc[pl.ds(FIRST, USED), :])
        for p in range(4):
            mask = masks[:, pl.ds(p * LANES, LANES)]
            picked[:, pl.ds(p * LANES, LANES)] = high * mask
            picked[:, pl.ds((p + 4) * LANES, LANES)] = low * mask
        across = lax.dot_general(perm[...], picked[...], NT, preferred_element_type=F32)
        extra = jnp.dot(across.astype(BF16), onehot[pl.ds(FIRST, USED), :], preferred_element_type=F32)
        extra = extra[0:64] + extra[64:128]
        cube = ref.reshape(EDGE, EDGE, EDGE, LANES)
        for f in range(6):
            more = extra[:, f * LANES : (f + 1) * LANES]
            if f < 2:
                ref[pl.ds(448 * f, 64), :] += more
            elif f < 4:
                cube[:, 7 * (f - 2)] += more.reshape(EDGE, EDGE, LANES)
            else:
                at = pl.ds(7 * (f - 4), 64, stride=EDGE)
                ref[at, :] = ref[at, :] + more

    await_all(9, block, n_p)
    keep.wait()
    for n in range(n_p):
        high, low = split(block[n])
        blocks[16 * n : 16 * n + 16, :] = high
        blocks[16 * (n_p + n) : 16 * (n_p + n) + 16, :] = low

    await_all(1, rc2, n_z)
    mine = jnp.sum(rc2[...], axis=0)
    high, low = split(jnp.concatenate([mine[0:1], mine[1:2]], axis=1))
    pair = jnp.concatenate([high.astype(F32), low.astype(F32), jnp.zeros((14, 2 * LANES), F32)], axis=0).astype(BF16)
    product = lax.dot_general(pair, blocks[...], NT, preferred_element_type=F32)
    count = 16 * n_p
    product = product[0:1, :count] + (product[1:2, :count] + product[0:1, count:])
    mine = jnp.concatenate([product[:, LANES * h : LANES * h + LANES] for h in range(4)], axis=0)
    own3[...] = mine
    rc3[me] = mine
    send_plane(lambda t: own3, rc3, 2)

    send_faces(field, out1, inc1, 7)

    await_all(2, rc3, n_p)
    mine = jnp.sum(rc3[...], axis=0)
    own4[...] = mine
    rc4[z] = mine
    send_line(own4, rc4, 3)
    await_faces(7, inc1)
    place_faces(field, inc1)
    loads["diag"].wait()
    loads["cross"].wait()

    await_all(3, rc4, n_z)
    for q in range(n_z):
        coarse[pl.ds(4 * q, 4), :] = rc4[q]

    high, low = split(coarse[...])
    at_low = jnp.dot(jnp.concatenate([high, low], axis=0), y_one[...], preferred_element_type=F32)
    corner = jnp.sum((at_low[0:64] + at_low[64:128]) * h_one[...], axis=0, keepdims=True)
    planes = []
    for ci in range(2):
        lines = []
        for cj in range(2):
            at = (4 * ci + 2 * cj) * LANES
            lines.append(hat_rows[0] * corner[:, at : at + LANES] + hat_rows[1] * corner[:, at + LANES : at + 2 * LANES])
        planes.append(
            jnp.concatenate(
                [float(HATS[0, j]) * lines[0] + float(HATS[1, j]) * lines[1] for j in range(EDGE)], axis=0
            )
        )
    for i in range(EDGE):
        at = pl.ds(64 * i, 64)
        lifted = float(HATS[0, i]) * planes[0] + float(HATS[1, i]) * planes[1]
        direction[at, :] = alive * (field[at, :] + lifted)

    def take(ref, start, stride):
        return [ref[pl.ds(pl.multiple_of(start + stride * m, 8), 8), :] for m in range(EDGE)]

    def along_first(j, c):
        result = mirrored(D_EVEN, D_ODD, take(direction, 8 * j, 64))
        for a in range(EDGE):
            grad1[pl.ds(pl.multiple_of(64 * a + 8 * j, 8), 8), :] = result[a]
        return c

    lax.fori_loop(0, EDGE, along_first, 0)

    def turn(values, ref):
        for m in range(EDGE):
            ref[pl.ds(EDGE * m, EDGE), :] = values[m]
        return [ref[pl.ds(m, EDGE, stride=EDGE), :] for m in range(EDGE)]

    def middle(i, sums):
        curve, dots = sums
        start = pl.multiple_of(64 * i, 64)
        slab = pl.ds(start, 64)
        d = take(direction, start, 8)
        across = turn(d, turned.at[pl.ds(0, 64)])
        g3 = turn(mirrored(D_EVEN, D_ODD, across), turned.at[pl.ds(64, 64)])
        g2 = mirrored(D_EVEN, D_ODD, d)
        g1 = take(grad1, start, 8)
        m = [diag[q, slab, :].astype(F32) for q in range(3)] + [cross[q, slab, :].astype(F32) for q in range(3)]
        f2, f3 = [], []
        for j in range(EDGE):
            rr, ss, tt, rs, rt, st = [q[8 * j : 8 * j + 8] for q in m]
            u = rr * g1[j] + rs * g2[j] + rt * g3[j]
            v = rs * g1[j] + ss * g2[j] + st * g3[j]
            w = rt * g1[j] + st * g2[j] + tt * g3[j]
            curve = curve + (g1[j] * u + g2[j] * v) + (g3[j] * w + d[j] * d[j])
            grad1[pl.ds(start + 8 * j, 8), :] = u
            f2.append(v)
            f3.append(w)
        dots = dots + jnp.sum((rm[slab, :] * direction[slab, :]).reshape(EDGE, EDGE, LANES), axis=0)
        b3 = turn(mirrored(T_EVEN, T_ODD, turn(f3, turned2.at[pl.ds(0, 64)])), turned2.at[pl.ds(64, 64)])
        b2 = mirrored(T_EVEN, T_ODD, f2)
        for j in range(EDGE):
            field[pl.ds(start + 8 * j, 8), :] = (b2[j] + b3[j]) + d[j]
        return curve, dots

    zero = jnp.zeros((EDGE, LANES), F32)
    curve, dots = lax.fori_loop(0, EDGE, middle, (zero, zero))

    def back_first(j, c):
        result = mirrored(T_EVEN, T_ODD, take(grad1, 8 * j, 64))
        for a in range(EDGE):
            at = pl.ds(pl.multiple_of(64 * a + 8 * j, 8), 8)
            field[at, :] = field[at, :] + result[a]
        return c

    lax.fori_loop(0, EDGE, back_first, 0)

    send_faces(field, out2, inc2, 8)

    def folded(a, b):
        return jnp.sum((a * b).reshape(POINTS // EDGE, EDGE, LANES), axis=0)

    old = folded(rm[...], rm[...])
    loads["sol"].wait()
    sol[...] = sol[...] * alive
    await_faces(8, inc2)
    place_faces(field, inc2)

    image = field[...]
    mixed = folded(rm[...], image)
    square = folded(image, image)
    sums = jnp.zeros((1, LANES), F32)
    for q, value in enumerate((dots, curve, old, mixed, square)):
        one = jnp.sum(jnp.sum(value, axis=0, keepdims=True), axis=1, keepdims=True)
        sums = jnp.where(lane == q, one, sums)
    own_a[...] = sums
    rc_a[me] = sums
    send_plane(lambda t: own_a, rc_a, 5)
    await_all(5, rc_a, n_p)
    sums = jnp.sum(rc_a[...], axis=0)
    own_b[...] = sums
    rc_b[z] = sums
    send_line(own_b, rc_b, 6)
    await_all(6, rc_b, n_z)
    sums = jnp.sum(rc_b[...], axis=0)

    totals[...] = sums
    for phase, some in sent:
        pltpu.make_async_copy(some, some, send_sem.at[phase]).wait()


def update(sol, res, direction, image, sums_ref, sol_out, res_out, ratio_out, moved, left, sem):
    lane = iota((1, LANES), 1)
    sums = sums_ref[...]

    def total(q):
        return jnp.sum(jnp.where(lane == q, sums, 0.0), axis=1, keepdims=True)

    step = total(0) / total(1)
    parts = 4
    rows = POINTS // parts
    stores = []
    for h in range(parts):
        at = pl.ds(rows * h, rows)
        for q, (ref, value, out) in enumerate(
            ((moved, sol[at, :] + step * direction[at, :], sol_out), (left, res[at, :] - step * image[at, :], res_out))
        ):
            ref[at, :] = value
            store = pltpu.make_async_copy(ref.at[at], out.at[at], sem.at[h, q])
            store.start()
            stores.append(store)
    ratio = (total(2) - 2.0 * step * total(3) + step * step * total(4)) / total(2)
    ratio_out[0] = jnp.sum(ratio)
    for store in stores:
        store.wait()


def on_device(n_x, n_y, *args):
    live, vid, eig, sface, scode, pface, pcode = (args[i] for i in (8, 6, 5, 9, 10, 11, 12))
    smem = pl.BlockSpec(memory_space=pltpu.SMEM)
    vmem = pl.BlockSpec(memory_space=pltpu.VMEM)
    hbm = pl.BlockSpec(memory_space=pl.ANY)
    n_p, n_z = 2 * n_y, n_x // 2
    field = pltpu.VMEM((POINTS, LANES), F32)
    whole = jax.ShapeDtypeStruct((POINTS, LANES), F32)
    held = [field] * 4 + [pltpu.VMEM((1, LANES), F32)]
    results = pl.pallas_call(
        functools.partial(kernel, n_x, n_y),
        out_shape=held,
        in_specs=[hbm] * 13,
        out_specs=[vmem] * 5,
        scratch_shapes=[
            pltpu.SMEM((1,), jnp.int32),
            pltpu.VMEM(vid.shape, jnp.int32),
            pltpu.VMEM(eig.shape, F32),
            pltpu.VMEM(sface.shape, jnp.int32),
            pltpu.VMEM(scode.shape, jnp.int32),
            pltpu.VMEM(pface.shape, jnp.int32),
            pltpu.VMEM(pcode.shape, jnp.int32),
            pltpu.VMEM((3, POINTS, LANES), BF16),
            pltpu.VMEM((3, POINTS, LANES), BF16),
            pltpu.VMEM((3, EDGE, EDGE, LANES), F32),
            pltpu.VMEM((n_p, 16, 2 * LANES), F32),
            pltpu.VMEM((32 * n_p, 2 * LANES), BF16),
            field,
            field,
            field,
            field,
            field,
            pltpu.VMEM((LANES, 8 * LANES), BF16),
            pltpu.VMEM((LANES, 8 * LANES), BF16),
            pltpu.VMEM((64, 8 * LANES), F32),
            pltpu.VMEM((n_p, 2, LANES), F32),
            pltpu.VMEM((n_p, 2, LANES), F32),
            pltpu.VMEM((2, LANES), F32),
            pltpu.VMEM((n_z, 2, LANES), F32),
            pltpu.VMEM((4, LANES), F32),
            pltpu.VMEM((n_p, 4, LANES), F32),
            pltpu.VMEM((4, LANES), F32),
            pltpu.VMEM((n_z, 4, LANES), F32),
            pltpu.VMEM((64, LANES), F32),
            pltpu.VMEM((ROWS, LANES), F32),
            pltpu.VMEM((USED, LANES), F32),
            pltpu.VMEM((ROWS, 6 * LANES), BF16),
            pltpu.VMEM((USED, 4 * LANES), BF16),
            pltpu.VMEM((LANES, 8 * LANES), BF16),
            pltpu.VMEM((LANES, 6 * LANES), BF16),
            pltpu.VMEM((ROWS, LANES), F32),
            pltpu.VMEM((ROWS, LANES), F32),
            pltpu.VMEM((ROWS, LANES), F32),
            pltpu.VMEM((ROWS, LANES), F32),
            pltpu.VMEM((USED, 8 * LANES), BF16),
            pltpu.VMEM((1, LANES), F32),
            pltpu.VMEM((n_p, 1, LANES), F32),
            pltpu.VMEM((1, LANES), F32),
            pltpu.VMEM((n_z, 1, LANES), F32),
            pltpu.SemaphoreType.REGULAR,
            pltpu.SemaphoreType.DMA((14,)),
            pltpu.SemaphoreType.DMA((10,)),
            pltpu.SemaphoreType.DMA((10,)),
        ],
        compiler_params=pltpu.CompilerParams(
            collective_id=0, has_side_effects=True, vmem_limit_bytes=60 * 1024 * 1024
        ),
    )(*args)
    return pl.pallas_call(
        update,
        out_shape=(whole, whole, jax.ShapeDtypeStruct((1,), F32)),
        in_specs=[vmem] * 5,
        out_specs=(hbm, hbm, smem),
        scratch_shapes=[field, field, pltpu.SemaphoreType.DMA((4, 2))],
        compiler_params=pltpu.CompilerParams(vmem_limit_bytes=60 * 1024 * 1024),
    )(*[pltpu.with_memory_space_constraint(r, pltpu.VMEM) for r in results])


def solution(mesh):
    both = ("gx", "gy")
    placed = (
        P(None, both),
        P(None, both),
        P(None, None, both),
        P(None, None, both),
        P(None, None, None, both),
        P(None, None, both),
        P(None, both),
        P(both, None),
        P(both),
        P(both, None, None),
        P(both, None, None),
        P(both, None, None),
        P(both, None, None),
    )
    return jax.shard_map(
        functools.partial(on_device, mesh.shape["gx"], mesh.shape["gy"]),
        mesh=mesh,
        in_specs=placed,
        out_specs=(P(None, both), P(None, both), P()),
        check_vma=False,
    )
```

```python
import functools

import numpy as np
import jax
import jax.numpy as jnp
from jax import lax
from jax.experimental import pallas as pl
from jax.experimental.pallas import tpu as pltpu
from jax.sharding import PartitionSpec as P

EDGE = 8
LANES = 128
POINTS = 512
F32 = jnp.float32
BF16 = jnp.bfloat16
MESH = pl.DeviceIdType.MESH
NT = (((1,), (1,)), ((), ()))

ROWS = 320
FIRST = 32
PEER_ROW = 64
PEER_ROWS = 24
SPARE = 184
PIPE_ROW = 192
PIPE_ROWS = 64
SENT_ROWS = 5 * PEER_ROWS + 2 * PIPE_ROWS
USED = ROWS - FIRST


def node_points():
    return -np.cos(np.pi * np.arange(EDGE) / (EDGE - 1))


def derivative_matrix():
    t = node_points()
    c = np.where((np.arange(EDGE) == 0) | (np.arange(EDGE) == EDGE - 1), 2.0, 1.0)
    d = np.zeros((EDGE, EDGE))
    for a in range(EDGE):
        for b in range(EDGE):
            if a != b:
                d[a, b] = c[a] / c[b] * (-1.0) ** (a + b) / (t[a] - t[b])
    for a in range(EDGE):
        d[a, a] = -np.sum(d[a])
    return d


def halves(matrix):
    front, back = matrix[:4, :4], matrix[:4, ::-1][:, :4]
    return (front + back) / 2, (front - back) / 2


D_EVEN, D_ODD = halves(derivative_matrix())
T_EVEN, T_ODD = halves(derivative_matrix().T)
HATS = np.stack([(1.0 - node_points()) / 2, (1.0 + node_points()) / 2])


def mirrored(even, odd, u):
    total = [u[m] + u[7 - m] for m in range(4)]
    apart = [u[m] - u[7 - m] for m in range(4)]
    front, back = [], []
    for a in range(4):
        e = float(even[a, 0]) * total[0]
        o = float(odd[a, 0]) * apart[0]
        for m in range(1, 4):
            e = e + float(even[a, m]) * total[m]
            o = o + float(odd[a, m]) * apart[m]
        front.append(o + e)
        back.append(o - e)
    return front + back[::-1]


def split(x):
    high = x.astype(BF16)
    return high, (x - high.astype(F32)).astype(BF16)


def iota(shape, dim):
    return lax.broadcasted_iota(jnp.int32, shape, dim)


def kernel(
    n_x,
    n_y,
    sol_hbm,
    res_hbm,
    diag_hbm,
    cross_hbm,
    fdm_hbm,
    eig_hbm,
    vid_hbm,
    inv_hbm,
    live_hbm,
    sface_hbm,
    scode_hbm,
    pface_hbm,
    pcode_hbm,
    sol,
    rm,
    direction,
    field,
    totals,
    live_ref,
    vid_ref,
    eig_ref,
    sface_ref,
    scode_ref,
    pface_ref,
    pcode_ref,
    diag,
    cross,
    fdm,
    block,
    blocks,
    buf_a,
    buf_b,
    turned,
    turned2,
    grad1,
    x_one,
    y_one,
    h_one,
    part,
    rc1,
    own2,
    rc2,
    own3,
    rc3,
    own4,
    rc4,
    coarse,
    idm,
    cdm,
    onehot,
    masks,
    perm,
    faces,
    out1,
    inc1,
    out2,
    inc2,
    picked,
    own_a,
    rc_a,
    own_b,
    rc_b,
    ready,
    in_sem,
    send_sem,
    recv_sem,
):
    x, y = lax.axis_index("gx"), lax.axis_index("gy")
    z, core = x // 2, lax.rem(x, 2)
    n_z, n_p = n_x // 2, 2 * n_y
    me = core * n_y + y
    offsets = (1, n_y - 1, 2, n_y - 2, n_y // 2)
    back_to = (1, 0, 3, 2, 4)

    moved = dict(
        live=(live_hbm, live_ref),
        residual=(res_hbm, rm),
        vid=(vid_hbm, vid_ref),
        sface=(sface_hbm, sface_ref),
        scode=(scode_hbm, scode_ref),
        pface=(pface_hbm, pface_ref),
        pcode=(pcode_hbm, pcode_ref),
        fdm=(fdm_hbm, fdm),
        eig=(eig_hbm, eig_ref),
        diag=(diag_hbm, diag),
        cross=(cross_hbm, cross),
        sol=(sol_hbm, sol),
    )
    loads = {n: pltpu.make_async_copy(s, d, in_sem.at[i]) for i, (n, (s, d)) in enumerate(moved.items())}
    barrier = pltpu.get_barrier_semaphore()

    def at_plane(k):
        k = k + k // 10
        a, b = y // 4 + 2 + k // 4, y + 2 + k
        return 4 * lax.rem(a, 4) + lax.rem(b, 4)

    def over_plane(act):
        def body(k, c):
            other = at_plane(k)
            for half in range(2):
                act(2 * z + half, other, half * n_y + other)
            return c

        lax.fori_loop(0, n_y - 1, body, 0)
        act(2 * z + 1 - core, y, (1 - core) * n_y + y)

    def over_line(act):
        def body(k, c):
            away = (k + 1) // 2
            act(lax.rem(z + n_z + n_z // 2 + away * (1 - 2 * lax.rem(k, 2)), n_z))
            return c

        lax.fori_loop(0, n_z - 1, body, 0)

    def at_device(i, j):
        return dict(device_id=(i, j), device_id_type=MESH)

    def greet_plane(k, c):
        pl.semaphore_signal(barrier, inc=1, **at_device(2 * z, at_plane(k)))
        return c

    lax.fori_loop(0, n_y - 1, greet_plane, 0)

    @pl.when(core == 1)
    def _():
        pl.semaphore_signal(barrier, inc=1, **at_device(2 * z, y))

    for load in loads.values():
        load.start()

    over_line(lambda t: pl.semaphore_signal(barrier, inc=1, **at_device(2 * t + 1, y)))

    sent = []

    def send(source, target, phase, i, j):
        pltpu.make_async_remote_copy(
            src_ref=source,
            dst_ref=target,
            send_sem=send_sem.at[phase],
            recv_sem=recv_sem.at[phase],
            **at_device(i, j),
        ).start()

    def send_plane(source, landing, phase):
        over_plane(lambda i, j, t: send(source(t), landing.at[me], phase, i, j))
        sent.append((phase, landing.at[pl.ds(0, n_p - 1)]))

    def send_line(source, landing, phase):
        over_line(lambda t: send(source, landing.at[z], phase, 2 * t + core, y))
        sent.append((phase, landing.at[pl.ds(0, n_z - 1)]))

    def await_all(phase, landing, n):
        some = landing.at[pl.ds(0, n - 1)]
        pltpu.make_async_copy(some, some, recv_sem.at[phase]).wait()

    loads["live"].wait()
    alive = (iota((1, LANES), 1) < live_ref[0]).astype(F32)
    lane = iota((1, LANES), 1)
    sub8 = iota((EDGE, 1), 0)
    hat_rows = []
    for c in range(2):
        h = jnp.zeros((EDGE, 1), F32)
        for k in range(EDGE):
            h = jnp.where(sub8 == k, float(HATS[c, k]), h)
        hat_rows.append(h)

    inc1[pl.ds(SPARE, 8), :] = jnp.zeros((8, LANES), F32)
    inc2[pl.ds(SPARE, 8), :] = jnp.zeros((8, LANES), F32)
    loads["residual"].wait()
    loads["vid"].wait()
    along_i = [None, None]
    for i in range(EDGE):
        slab = rm[pl.ds(64 * i, 64), :] * alive
        rm[pl.ds(64 * i, 64), :] = slab
        for c in range(2):
            term = float(HATS[c, i]) * slab
            along_i[c] = term if i == 0 else along_i[c] + term
    high_iota = iota((64, LANES), 0)
    low_iota = iota((LANES, LANES), 0)
    for ci in range(2):
        for cj in range(2):
            plane = float(HATS[cj, 0]) * along_i[ci][0:8]
            for j in range(1, EDGE):
                plane = plane + float(HATS[cj, j]) * along_i[ci][8 * j : 8 * j + 8]
            for ck in range(2):
                c = 4 * ci + 2 * cj + ck
                value = jnp.sum(plane * hat_rows[ck], axis=0, keepdims=True)
                ids = vid_ref[c : c + 1, :]
                at = pl.ds(c * LANES, LANES)
                here = (high_iota == (ids >> 7)).astype(F32)
                h_one[:, at] = here
                high, low = split(here * value)
                x_one[0:64, at] = high
                x_one[64:128, at] = low
                y_one[:, at] = (low_iota == (ids & 127)).astype(F32).astype(BF16)
    both = lax.dot_general(x_one[...], y_one[...], NT, preferred_element_type=F32)
    partial = both[0:64] + both[64:128]
    for q in range(n_p):
        part[q] = partial[2 * q : 2 * q + 2]

    @pl.when(core == 0)
    def _():
        pl.semaphore_wait(barrier, n_p - 1)
        pl.semaphore_signal(ready, inc=1, **at_device(2 * z + 1, y))

    @pl.when(core == 1)
    def _():
        pl.semaphore_wait(ready, 1)

    send_plane(lambda t: part.at[t], rc1, 0)
    rc1[me] = part[me]
    send_plane(lambda t: inv_hbm.at[:, pl.ds(pl.multiple_of(256 * t, 256), 256)], block, 9)
    keep = pltpu.make_async_copy(inv_hbm.at[:, pl.ds(pl.multiple_of(256 * me, 256), 256)], block.at[me], in_sem.at[13])
    keep.start()

    def column(row, rows, swap=0):
        width = row.shape[1]
        diagonal = (iota((rows, width), 0) ^ swap) == iota((rows, width), 1)
        kept = jnp.where(diagonal, row.astype(F32) + 1.0, 0.0)
        return jnp.broadcast_to(jnp.sum(kept, axis=1, keepdims=True) - 1.0, (rows, LANES))

    for name in ("sface", "scode", "pface", "pcode"):
        loads[name].wait()
    idm[pl.ds(0, 32), :] = column(sface_ref[0, pl.ds(y, 1), :], 32, 1)
    idm[pl.ds(32, 32), :] = column(sface_ref[0, pl.ds(y, 1), :], 32)
    cdm[pl.ds(0, 32), :] = column(scode_ref[0, pl.ds(y, 1), :], 32)
    for g in range(5):
        peer = lax.rem(y + offsets[g], n_y)
        at = PEER_ROW + PEER_ROWS * g
        idm[pl.ds(at, PEER_ROWS), :] = column(sface_ref[0, pl.ds(peer, 1), :], PEER_ROWS)
        cdm[pl.ds(at - FIRST, PEER_ROWS), :] = column(scode_ref[0, pl.ds(peer, 1), :], PEER_ROWS)
    idm[pl.ds(SPARE, 8), :] = jnp.full((8, LANES), -1.0, F32)
    cdm[pl.ds(SPARE - FIRST, 8), :] = jnp.full((8, LANES), -1.0, F32)
    for s in range(2):
        at = PIPE_ROW + PIPE_ROWS * s
        idm[pl.ds(at, PIPE_ROWS), :] = column(pface_ref[0, s : s + 1, :], PIPE_ROWS)
        cdm[pl.ds(at - FIRST, PIPE_ROWS), :] = column(pcode_ref[0, s : s + 1, :], PIPE_ROWS)
    ids = idm[...]
    for f in range(6):
        onehot[:, pl.ds(f * LANES, LANES)] = (ids == (6 * lane + f).astype(F32)).astype(F32).astype(BF16)
    codes = cdm[...]
    half = (lane >> 6).astype(F32)
    for p in range(4):
        masks[:, pl.ds(p * LANES, LANES)] = (codes == 2.0 * p + half).astype(F32).astype(BF16)
    grid_row = iota((LANES, LANES), 0)
    grid_lane = iota((LANES, LANES), 1)
    first, second = (grid_row & 63) >> 3, grid_row & 7
    flip = 7 * (grid_lane >> 6)
    for t in range(8):
        a, b = (second, first) if t % 4 >= 2 else (first, second)
        b = b ^ 7 if t % 2 == 1 else b
        source = 8 * (a ^ flip) + b
        fits = (source == (grid_lane & 63)) & ((grid_row < 64) if t < 4 else (grid_row >= 64))
        perm[:, pl.ds(t * LANES, LANES)] = fits.astype(F32).astype(BF16)

    await_all(0, rc1, n_p)
    mine = jnp.sum(rc1[...], axis=0)
    own2[...] = mine
    rc2[z] = mine

    @pl.when(core == 1)
    def _():
        pl.semaphore_wait(barrier, 2 * (n_z - 1))
        pl.semaphore_signal(ready, inc=1, **at_device(2 * z, y))

    @pl.when(core == 0)
    def _():
        pl.semaphore_wait(ready, 1)

    send_line(own2, rc2, 1)

    def sum_of(coef, slabs, a):
        total = coef(0, a) * slabs(0)
        for m in range(1, EDGE):
            total = total + coef(m, a) * slabs(m)
        return total

    def per_row(body):
        def step(a, c):
            body(a)
            return c

        lax.fori_loop(0, EDGE, step, 0)

    def slab_i(ref):
        return lambda m: ref[pl.ds(pl.multiple_of(64 * m, 64), 64), :]

    def slab_j(ref):
        cube = ref.reshape(EDGE, EDGE, EDGE, LANES)
        return lambda m: cube[:, m].reshape(64, LANES)

    def forward(d):
        return lambda m, a: fdm[d, m, pl.ds(a, 1), :]

    def backward(d):
        return lambda m, a: fdm[d, a, m : m + 1, :]

    def put_i(ref, a, value):
        ref[pl.ds(pl.multiple_of(64 * a, 64), 64), :] = value

    def put_j(ref, a, value):
        ref.reshape(EDGE, EDGE, EDGE, LANES)[:, pl.ds(a, 1)] = value.reshape(EDGE, 1, EDGE, LANES)

    loads["fdm"].wait()
    loads["eig"].wait()
    per_row(lambda a: put_i(buf_a, a, sum_of(forward(0), slab_i(rm), a)))
    per_row(lambda a: put_j(buf_b, a, sum_of(forward(1), slab_j(buf_a), a)))
    for k in range(EDGE):
        turned[pl.ds(64 * k, 64), :] = buf_b[pl.ds(k, 64, stride=EDGE), :]
    base = jnp.concatenate([eig_ref[0, a : a + 1, :] + eig_ref[1] for a in range(EDGE)], axis=0)
    buf_a[pl.ds(0, 64), :] = base

    def spectral(a):
        value = sum_of(forward(2), slab_i(turned), a)
        put_i(buf_b, a, value / (buf_a[pl.ds(0, 64), :] + eig_ref[2, pl.ds(a, 1), :]))

    per_row(spectral)

    per_row(lambda a: put_i(turned, a, sum_of(backward(2), slab_i(buf_b), a)))
    for k in range(EDGE):
        buf_a[pl.ds(k, 64, stride=EDGE), :] = turned[pl.ds(64 * k, 64), :]
    per_row(lambda a: put_j(buf_b, a, sum_of(backward(1), slab_j(buf_a), a)))
    per_row(lambda a: put_i(field, a, sum_of(backward(0), slab_i(buf_b), a)))

    def face_of(ref, f):
        if f < 2:
            return ref[pl.ds(448 * f, 64), :]
        if f < 4:
            return slab_j(ref)(7 * (f - 2))
        return ref[pl.ds(7 * (f - 4), 64, stride=EDGE), :]

    def send_faces(ref, out, inc, phase):
        for f in range(6):
            high, low = split(face_of(ref, f))
            faces[0:64, pl.ds(f * LANES, LANES)] = high
            faces[64:128, pl.ds(f * LANES, LANES)] = low
        found = lax.dot_general(onehot[...], faces[...], NT, preferred_element_type=F32)
        found = found + pltpu.roll(found, 64, 1)
        out[...] = found
        inc[pl.ds(FIRST, 32), :] = found[0:32]
        hops = [
            (
                PIPE_ROW + PIPE_ROWS * s,
                PIPE_ROW + PIPE_ROWS * (1 - s),
                PIPE_ROWS,
                (lax.rem(x + n_x - 1 + 2 * s, n_x), y),
            )
            for s in range(2)
        ] + [
            (
                PEER_ROW + PEER_ROWS * g,
                PEER_ROW + PEER_ROWS * back_to[g],
                PEER_ROWS,
                (x, lax.rem(y + offsets[g], n_y)),
            )
            for g in range(5)
        ]
        for start, land, count, target in hops:
            send(out.at[pl.ds(start, count)], inc.at[pl.ds(land, count)], phase, *target)
        sent.append((phase, inc.at[pl.ds(0, SENT_ROWS)]))

    def await_faces(phase, inc):
        some = inc.at[pl.ds(0, SENT_ROWS)]
        pltpu.make_async_copy(some, some, recv_sem.at[phase]).wait()

    def place_faces(ref, inc):
        high, low = split(inc[pl.ds(FIRST, USED), :])
        for p in range(4):
            mask = masks[:, pl.ds(p * LANES, LANES)]
            picked[:, pl.ds(p * LANES, LANES)] = high * mask
            picked[:, pl.ds((p + 4) * LANES, LANES)] = low * mask
        across = lax.dot_general(perm[...], picked[...], NT, preferred_element_type=F32)
        extra = jnp.dot(across.astype(BF16), onehot[pl.ds(FIRST, USED), :], preferred_element_type=F32)
        extra = extra[0:64] + extra[64:128]
        cube = ref.reshape(EDGE, EDGE, EDGE, LANES)
        for f in range(6):
            more = extra[:, f * LANES : (f + 1) * LANES]
            if f < 2:
                ref[pl.ds(448 * f, 64), :] += more
            elif f < 4:
                cube[:, 7 * (f - 2)] += more.reshape(EDGE, EDGE, LANES)
            else:
                at = pl.ds(7 * (f - 4), 64, stride=EDGE)
                ref[at, :] = ref[at, :] + more

    await_all(9, block, n_p)
    keep.wait()
    for n in range(n_p):
        high, low = split(block[n])
        blocks[16 * n : 16 * n + 16, :] = high
        blocks[16 * (n_p + n) : 16 * (n_p + n) + 16, :] = low

    await_all(1, rc2, n_z)
    mine = jnp.sum(rc2[...], axis=0)
    high, low = split(jnp.concatenate([mine[0:1], mine[1:2]], axis=1))
    pair = jnp.concatenate([high.astype(F32), low.astype(F32), jnp.zeros((14, 2 * LANES), F32)], axis=0).astype(BF16)
    product = lax.dot_general(pair, blocks[...], NT, preferred_element_type=F32)
    count = 16 * n_p
    product = product[0:1, :count] + (product[1:2, :count] + product[0:1, count:])
    mine = jnp.concatenate([product[:, LANES * h : LANES * h + LANES] for h in range(4)], axis=0)
    own3[...] = mine
    rc3[me] = mine
    send_plane(lambda t: own3, rc3, 2)

    send_faces(field, out1, inc1, 7)

    await_all(2, rc3, n_p)
    mine = jnp.sum(rc3[...], axis=0)
    own4[...] = mine
    rc4[z] = mine
    send_line(own4, rc4, 3)
    await_faces(7, inc1)
    place_faces(field, inc1)
    loads["diag"].wait()
    loads["cross"].wait()

    await_all(3, rc4, n_z)
    for q in range(n_z):
        coarse[pl.ds(4 * q, 4), :] = rc4[q]

    high, low = split(coarse[...])
    at_low = jnp.dot(jnp.concatenate([high, low], axis=0), y_one[...], preferred_element_type=F32)
    corner = jnp.sum((at_low[0:64] + at_low[64:128]) * h_one[...], axis=0, keepdims=True)
    planes = []
    for ci in range(2):
        lines = []
        for cj in range(2):
            at = (4 * ci + 2 * cj) * LANES
            lines.append(hat_rows[0] * corner[:, at : at + LANES] + hat_rows[1] * corner[:, at + LANES : at + 2 * LANES])
        planes.append(
            jnp.concatenate(
                [float(HATS[0, j]) * lines[0] + float(HATS[1, j]) * lines[1] for j in range(EDGE)], axis=0
            )
        )
    for i in range(EDGE):
        at = pl.ds(64 * i, 64)
        lifted = float(HATS[0, i]) * planes[0] + float(HATS[1, i]) * planes[1]
        direction[at, :] = alive * (field[at, :] + lifted)

    def take(ref, start, stride):
        return [ref[pl.ds(start + stride * m, 8), :] for m in range(EDGE)]

    def along_first(j, c):
        result = mirrored(D_EVEN, D_ODD, take(direction, 8 * j, 64))
        for a in range(EDGE):
            grad1[pl.ds(64 * a + 8 * j, 8), :] = result[a]
        return c

    for j in range(EDGE):
        along_first(j, 0)

    def turn(values, ref):
        for m in range(EDGE):
            ref[pl.ds(EDGE * m, EDGE), :] = values[m]
        return [ref[pl.ds(m, EDGE, stride=EDGE), :] for m in range(EDGE)]

    def middle(i, sums):
        curve, dots = sums
        start = 64 * i
        slab = pl.ds(start, 64)
        d = take(direction, start, 8)
        across = turn(d, turned.at[slab])
        g3 = turn(mirrored(D_EVEN, D_ODD, across), turned2.at[slab])
        g2 = mirrored(D_EVEN, D_ODD, d)
        g1 = take(grad1, start, 8)
        m = [diag[q, slab, :].astype(F32) for q in range(3)] + [cross[q, slab, :].astype(F32) for q in range(3)]
        f2, f3 = [], []
        for j in range(EDGE):
            rr, ss, tt, rs, rt, st = [q[8 * j : 8 * j + 8] for q in m]
            u = rr * g1[j] + rs * g2[j] + rt * g3[j]
            v = rs * g1[j] + ss * g2[j] + st * g3[j]
            w = rt * g1[j] + st * g2[j] + tt * g3[j]
            curve = curve + (g1[j] * u + g2[j] * v) + (g3[j] * w + d[j] * d[j])
            grad1[pl.ds(start + 8 * j, 8), :] = u
            f2.append(v)
            f3.append(w)
        dots = dots + jnp.sum((rm[slab, :] * direction[slab, :]).reshape(EDGE, EDGE, LANES), axis=0)
        b3 = turn(mirrored(T_EVEN, T_ODD, turn(f3, buf_a.at[slab])), buf_b.at[slab])
        b2 = mirrored(T_EVEN, T_ODD, f2)
        for j in range(EDGE):
            field[pl.ds(start + 8 * j, 8), :] = (b2[j] + b3[j]) + d[j]
        return curve, dots

    zero = jnp.zeros((EDGE, LANES), F32)
    sums = (zero, zero)
    for i in range(EDGE):
        sums = middle(i, sums)
    curve, dots = sums

    def back_first(j, c):
        result = mirrored(T_EVEN, T_ODD, take(grad1, 8 * j, 64))
        for a in range(EDGE):
            at = pl.ds(64 * a + 8 * j, 8)
            field[at, :] = field[at, :] + result[a]
        return c

    for j in range(EDGE):
        back_first(j, 0)

    send_faces(field, out2, inc2, 8)

    def folded(a, b):
        return jnp.sum((a * b).reshape(POINTS // EDGE, EDGE, LANES), axis=0)

    old = folded(rm[...], rm[...])
    loads["sol"].wait()
    sol[...] = sol[...] * alive
    await_faces(8, inc2)
    place_faces(field, inc2)

    image = field[...]
    mixed = folded(rm[...], image)
    square = folded(image, image)
    sums = jnp.zeros((1, LANES), F32)
    for q, value in enumerate((dots, curve, old, mixed, square)):
        one = jnp.sum(jnp.sum(value, axis=0, keepdims=True), axis=1, keepdims=True)
        sums = jnp.where(lane == q, one, sums)
    own_a[...] = sums
    rc_a[me] = sums
    send_plane(lambda t: own_a, rc_a, 5)
    await_all(5, rc_a, n_p)
    sums = jnp.sum(rc_a[...], axis=0)
    own_b[...] = sums
    rc_b[z] = sums
    send_line(own_b, rc_b, 6)
    await_all(6, rc_b, n_z)
    sums = jnp.sum(rc_b[...], axis=0)

    totals[...] = sums
    for phase, some in sent:
        pltpu.make_async_copy(some, some, send_sem.at[phase]).wait()


def update(sol, res, direction, image, sums_ref, sol_out, res_out, ratio_out, moved, left, sem):
    lane = iota((1, LANES), 1)
    sums = sums_ref[...]

    def total(q):
        return jnp.sum(jnp.where(lane == q, sums, 0.0), axis=1, keepdims=True)

    step = total(0) / total(1)
    parts = 4
    rows = POINTS // parts
    stores = []
    for h in range(parts):
        at = pl.ds(rows * h, rows)
        for q, (ref, value, out) in enumerate(
            ((moved, sol[at, :] + step * direction[at, :], sol_out), (left, res[at, :] - step * image[at, :], res_out))
        ):
            ref[at, :] = value
            store = pltpu.make_async_copy(ref.at[at], out.at[at], sem.at[h, q])
            store.start()
            stores.append(store)
    ratio = (total(2) - 2.0 * step * total(3) + step * step * total(4)) / total(2)
    ratio_out[0] = jnp.sum(ratio)
    for store in stores:
        store.wait()


def on_device(n_x, n_y, *args):
    live, vid, eig, sface, scode, pface, pcode = (args[i] for i in (8, 6, 5, 9, 10, 11, 12))
    smem = pl.BlockSpec(memory_space=pltpu.SMEM)
    vmem = pl.BlockSpec(memory_space=pltpu.VMEM)
    hbm = pl.BlockSpec(memory_space=pl.ANY)
    n_p, n_z = 2 * n_y, n_x // 2
    field = pltpu.VMEM((POINTS, LANES), F32)
    whole = jax.ShapeDtypeStruct((POINTS, LANES), F32)
    held = [field] * 4 + [pltpu.VMEM((1, LANES), F32)]
    results = pl.pallas_call(
        functools.partial(kernel, n_x, n_y),
        out_shape=held,
        in_specs=[hbm] * 13,
        out_specs=[vmem] * 5,
        scratch_shapes=[
            pltpu.SMEM((1,), jnp.int32),
            pltpu.VMEM(vid.shape, jnp.int32),
            pltpu.VMEM(eig.shape, F32),
            pltpu.VMEM(sface.shape, jnp.int32),
            pltpu.VMEM(scode.shape, jnp.int32),
            pltpu.VMEM(pface.shape, jnp.int32),
            pltpu.VMEM(pcode.shape, jnp.int32),
            pltpu.VMEM((3, POINTS, LANES), BF16),
            pltpu.VMEM((3, POINTS, LANES), BF16),
            pltpu.VMEM((3, EDGE, EDGE, LANES), F32),
            pltpu.VMEM((n_p, 16, 2 * LANES), F32),
            pltpu.VMEM((32 * n_p, 2 * LANES), BF16),
            field,
            field,
            field,
            field,
            field,
            pltpu.VMEM((LANES, 8 * LANES), BF16),
            pltpu.VMEM((LANES, 8 * LANES), BF16),
            pltpu.VMEM((64, 8 * LANES), F32),
            pltpu.VMEM((n_p, 2, LANES), F32),
            pltpu.VMEM((n_p, 2, LANES), F32),
            pltpu.VMEM((2, LANES), F32),
            pltpu.VMEM((n_z, 2, LANES), F32),
            pltpu.VMEM((4, LANES), F32),
            pltpu.VMEM((n_p, 4, LANES), F32),
            pltpu.VMEM((4, LANES), F32),
            pltpu.VMEM((n_z, 4, LANES), F32),
            pltpu.VMEM((64, LANES), F32),
            pltpu.VMEM((ROWS, LANES), F32),
            pltpu.VMEM((USED, LANES), F32),
            pltpu.VMEM((ROWS, 6 * LANES), BF16),
            pltpu.VMEM((USED, 4 * LANES), BF16),
            pltpu.VMEM((LANES, 8 * LANES), BF16),
            pltpu.VMEM((LANES, 6 * LANES), BF16),
            pltpu.VMEM((ROWS, LANES), F32),
            pltpu.VMEM((ROWS, LANES), F32),
            pltpu.VMEM((ROWS, LANES), F32),
            pltpu.VMEM((ROWS, LANES), F32),
            pltpu.VMEM((USED, 8 * LANES), BF16),
            pltpu.VMEM((1, LANES), F32),
            pltpu.VMEM((n_p, 1, LANES), F32),
            pltpu.VMEM((1, LANES), F32),
            pltpu.VMEM((n_z, 1, LANES), F32),
            pltpu.SemaphoreType.REGULAR,
            pltpu.SemaphoreType.DMA((14,)),
            pltpu.SemaphoreType.DMA((10,)),
            pltpu.SemaphoreType.DMA((10,)),
        ],
        compiler_params=pltpu.CompilerParams(
            collective_id=0, has_side_effects=True, vmem_limit_bytes=60 * 1024 * 1024
        ),
    )(*args)
    return pl.pallas_call(
        update,
        out_shape=(whole, whole, jax.ShapeDtypeStruct((1,), F32)),
        in_specs=[vmem] * 5,
        out_specs=(hbm, hbm, smem),
        scratch_shapes=[field, field, pltpu.SemaphoreType.DMA((4, 2))],
        compiler_params=pltpu.CompilerParams(vmem_limit_bytes=60 * 1024 * 1024),
    )(*[pltpu.with_memory_space_constraint(r, pltpu.VMEM) for r in results])


def solution(mesh):
    both = ("gx", "gy")
    placed = (
        P(None, both),
        P(None, both),
        P(None, None, both),
        P(None, None, both),
        P(None, None, None, both),
        P(None, None, both),
        P(None, both),
        P(both, None),
        P(both),
        P(both, None, None),
        P(both, None, None),
        P(both, None, None),
        P(both, None, None),
    )
    return jax.shard_map(
        functools.partial(on_device, mesh.shape["gx"], mesh.shape["gy"]),
        mesh=mesh,
        in_specs=placed,
        out_specs=(P(None, both), P(None, both), P()),
        check_vma=False,
    )
```

```python
import functools

import numpy as np
import jax
import jax.numpy as jnp
from jax import lax
from jax.experimental import pallas as pl
from jax.experimental.pallas import tpu as pltpu
from jax.sharding import PartitionSpec as P

EDGE = 8
LANES = 128
POINTS = 512
F32 = jnp.float32
BF16 = jnp.bfloat16
MESH = pl.DeviceIdType.MESH
NT = (((1,), (1,)), ((), ()))

ROWS = 320
FIRST = 32
PEER_ROW = 64
PEER_ROWS = 24
SPARE = 184
PIPE_ROW = 192
PIPE_ROWS = 64
SENT_ROWS = 5 * PEER_ROWS + 2 * PIPE_ROWS
USED = ROWS - FIRST


def node_points():
    return -np.cos(np.pi * np.arange(EDGE) / (EDGE - 1))


def derivative_matrix():
    t = node_points()
    c = np.where((np.arange(EDGE) == 0) | (np.arange(EDGE) == EDGE - 1), 2.0, 1.0)
    d = np.zeros((EDGE, EDGE))
    for a in range(EDGE):
        for b in range(EDGE):
            if a != b:
                d[a, b] = c[a] / c[b] * (-1.0) ** (a + b) / (t[a] - t[b])
    for a in range(EDGE):
        d[a, a] = -np.sum(d[a])
    return d


def halves(matrix):
    front, back = matrix[:4, :4], matrix[:4, ::-1][:, :4]
    return (front + back) / 2, (front - back) / 2


D_EVEN, D_ODD = halves(derivative_matrix())
T_EVEN, T_ODD = halves(derivative_matrix().T)
HATS = np.stack([(1.0 - node_points()) / 2, (1.0 + node_points()) / 2])


def mirrored(even, odd, u):
    total = [u[m] + u[7 - m] for m in range(4)]
    apart = [u[m] - u[7 - m] for m in range(4)]
    front, back = [], []
    for a in range(4):
        e = float(even[a, 0]) * total[0]
        o = float(odd[a, 0]) * apart[0]
        for m in range(1, 4):
            e = e + float(even[a, m]) * total[m]
            o = o + float(odd[a, m]) * apart[m]
        front.append(o + e)
        back.append(o - e)
    return front + back[::-1]


def split(x):
    high = x.astype(BF16)
    return high, (x - high.astype(F32)).astype(BF16)


def iota(shape, dim):
    return lax.broadcasted_iota(jnp.int32, shape, dim)


def kernel(
    n_x,
    n_y,
    sol_hbm,
    res_hbm,
    diag_hbm,
    cross_hbm,
    fdm_hbm,
    eig_hbm,
    vid_hbm,
    inv_hbm,
    live_hbm,
    sface_hbm,
    scode_hbm,
    pface_hbm,
    pcode_hbm,
    sol,
    rm,
    direction,
    field,
    totals,
    live_ref,
    vid_ref,
    eig_ref,
    sface_ref,
    scode_ref,
    pface_ref,
    pcode_ref,
    diag,
    cross,
    fdm,
    block,
    blocks,
    buf_a,
    buf_b,
    turned,
    turned2,
    grad1,
    x_one,
    y_one,
    h_one,
    part,
    rc1,
    own2,
    rc2,
    own3,
    rc3,
    own4,
    rc4,
    coarse,
    idm,
    cdm,
    onehot,
    masks,
    perm,
    faces,
    out1,
    inc1,
    out2,
    inc2,
    picked,
    own_a,
    rc_a,
    own_b,
    rc_b,
    ready,
    in_sem,
    send_sem,
    recv_sem,
):
    x, y = lax.axis_index("gx"), lax.axis_index("gy")
    z, core = x // 2, lax.rem(x, 2)
    n_z, n_p = n_x // 2, 2 * n_y
    me = core * n_y + y
    offsets = (1, n_y - 1, 2, n_y - 2, n_y // 2)
    back_to = (1, 0, 3, 2, 4)

    moved = dict(
        live=(live_hbm, live_ref),
        residual=(res_hbm, rm),
        vid=(vid_hbm, vid_ref),
        sface=(sface_hbm, sface_ref),
        scode=(scode_hbm, scode_ref),
        pface=(pface_hbm, pface_ref),
        pcode=(pcode_hbm, pcode_ref),
        fdm=(fdm_hbm, fdm),
        eig=(eig_hbm, eig_ref),
        diag=(diag_hbm, diag),
        cross=(cross_hbm, cross),
        sol=(sol_hbm, sol),
    )
    loads = {n: pltpu.make_async_copy(s, d, in_sem.at[i]) for i, (n, (s, d)) in enumerate(moved.items())}
    for load in loads.values():
        load.start()

    barrier = pltpu.get_barrier_semaphore()

    def at_plane(k):
        k = k + k // 10
        a, b = y // 4 + 2 + k // 4, y + 2 + k
        return 4 * lax.rem(a, 4) + lax.rem(b, 4)

    def over_plane(act):
        def body(k, c):
            other = at_plane(k)
            for half in range(2):
                act(2 * z + half, other, half * n_y + other)
            return c

        lax.fori_loop(0, n_y - 1, body, 0)
        act(2 * z + 1 - core, y, (1 - core) * n_y + y)

    def over_line(act):
        def body(k, c):
            away = (k + 1) // 2
            act(lax.rem(z + n_z + n_z // 2 + away * (1 - 2 * lax.rem(k, 2)), n_z))
            return c

        lax.fori_loop(0, n_z - 1, body, 0)

    def at_device(i, j):
        return dict(device_id=(i, j), device_id_type=MESH)

    def greet_plane(k, c):
        pl.semaphore_signal(barrier, inc=1, **at_device(2 * z, at_plane(k)))
        return c

    lax.fori_loop(0, n_y - 1, greet_plane, 0)

    @pl.when(core == 1)
    def _():
        pl.semaphore_signal(barrier, inc=1, **at_device(2 * z, y))

    over_line(lambda t: pl.semaphore_signal(barrier, inc=1, **at_device(2 * t + 1, y)))

    sent = []

    def send(source, target, phase, i, j):
        pltpu.make_async_remote_copy(
            src_ref=source,
            dst_ref=target,
            send_sem=send_sem.at[phase],
            recv_sem=recv_sem.at[phase],
            **at_device(i, j),
        ).start()

    def send_plane(source, landing, phase):
        over_plane(lambda i, j, t: send(source(t), landing.at[me], phase, i, j))
        sent.append((phase, landing.at[pl.ds(0, n_p - 1)]))

    def send_line(source, landing, phase):
        over_line(lambda t: send(source, landing.at[z], phase, 2 * t + core, y))
        sent.append((phase, landing.at[pl.ds(0, n_z - 1)]))

    def await_all(phase, landing, n):
        some = landing.at[pl.ds(0, n - 1)]
        pltpu.make_async_copy(some, some, recv_sem.at[phase]).wait()

    loads["live"].wait()
    alive = (iota((1, LANES), 1) < live_ref[0]).astype(F32)
    lane = iota((1, LANES), 1)
    sub8 = iota((EDGE, 1), 0)
    hat_rows = []
    for c in range(2):
        h = jnp.zeros((EDGE, 1), F32)
        for k in range(EDGE):
            h = jnp.where(sub8 == k, float(HATS[c, k]), h)
        hat_rows.append(h)

    inc1[pl.ds(SPARE, 8), :] = jnp.zeros((8, LANES), F32)
    inc2[pl.ds(SPARE, 8), :] = jnp.zeros((8, LANES), F32)
    loads["residual"].wait()
    loads["vid"].wait()
    along_i = [None, None]
    for i in range(EDGE):
        slab = rm[pl.ds(64 * i, 64), :] * alive
        rm[pl.ds(64 * i, 64), :] = slab
        for c in range(2):
            term = float(HATS[c, i]) * slab
            along_i[c] = term if i == 0 else along_i[c] + term
    high_iota = iota((64, LANES), 0)
    low_iota = iota((LANES, LANES), 0)
    for ci in range(2):
        for cj in range(2):
            plane = float(HATS[cj, 0]) * along_i[ci][0:8]
            for j in range(1, EDGE):
                plane = plane + float(HATS[cj, j]) * along_i[ci][8 * j : 8 * j + 8]
            for ck in range(2):
                c = 4 * ci + 2 * cj + ck
                value = jnp.sum(plane * hat_rows[ck], axis=0, keepdims=True)
                ids = vid_ref[c : c + 1, :]
                at = pl.ds(c * LANES, LANES)
                here = (high_iota == (ids >> 7)).astype(F32)
                h_one[:, at] = here
                high, low = split(here * value)
                x_one[0:64, at] = high
                x_one[64:128, at] = low
                y_one[:, at] = (low_iota == (ids & 127)).astype(F32).astype(BF16)
    both = lax.dot_general(x_one[...], y_one[...], NT, preferred_element_type=F32)
    partial = both[0:64] + both[64:128]
    for q in range(n_p):
        part[q] = partial[2 * q : 2 * q + 2]

    @pl.when(core == 0)
    def _():
        pl.semaphore_wait(barrier, n_p - 1)
        pl.semaphore_signal(ready, inc=1, **at_device(2 * z + 1, y))

    @pl.when(core == 1)
    def _():
        pl.semaphore_wait(ready, 1)

    send_plane(lambda t: part.at[t], rc1, 0)
    rc1[me] = part[me]
    send_plane(lambda t: inv_hbm.at[:, pl.ds(pl.multiple_of(256 * t, 256), 256)], block, 9)
    keep = pltpu.make_async_copy(inv_hbm.at[:, pl.ds(pl.multiple_of(256 * me, 256), 256)], block.at[me], in_sem.at[13])
    keep.start()

    def column(row, rows, swap=0):
        width = row.shape[1]
        diagonal = (iota((rows, width), 0) ^ swap) == iota((rows, width), 1)
        kept = jnp.where(diagonal, row.astype(F32) + 1.0, 0.0)
        return jnp.broadcast_to(jnp.sum(kept, axis=1, keepdims=True) - 1.0, (rows, LANES))

    for name in ("sface", "scode", "pface", "pcode"):
        loads[name].wait()
    idm[pl.ds(0, 32), :] = column(sface_ref[0, pl.ds(y, 1), :], 32, 1)
    idm[pl.ds(32, 32), :] = column(sface_ref[0, pl.ds(y, 1), :], 32)
    cdm[pl.ds(0, 32), :] = column(scode_ref[0, pl.ds(y, 1), :], 32)
    for g in range(5):
        peer = lax.rem(y + offsets[g], n_y)
        at = PEER_ROW + PEER_ROWS * g
        idm[pl.ds(at, PEER_ROWS), :] = column(sface_ref[0, pl.ds(peer, 1), :], PEER_ROWS)
        cdm[pl.ds(at - FIRST, PEER_ROWS), :] = column(scode_ref[0, pl.ds(peer, 1), :], PEER_ROWS)
    idm[pl.ds(SPARE, 8), :] = jnp.full((8, LANES), -1.0, F32)
    cdm[pl.ds(SPARE - FIRST, 8), :] = jnp.full((8, LANES), -1.0, F32)
    for s in range(2):
        at = PIPE_ROW + PIPE_ROWS * s
        idm[pl.ds(at, PIPE_ROWS), :] = column(pface_ref[0, s : s + 1, :], PIPE_ROWS)
        cdm[pl.ds(at - FIRST, PIPE_ROWS), :] = column(pcode_ref[0, s : s + 1, :], PIPE_ROWS)
    ids = idm[...]
    for f in range(6):
        onehot[:, pl.ds(f * LANES, LANES)] = (ids == (6 * lane + f).astype(F32)).astype(F32).astype(BF16)
    codes = cdm[...]
    half = (lane >> 6).astype(F32)
    for p in range(4):
        masks[:, pl.ds(p * LANES, LANES)] = (codes == 2.0 * p + half).astype(F32).astype(BF16)
    grid_row = iota((LANES, LANES), 0)
    grid_lane = iota((LANES, LANES), 1)
    first, second = (grid_row & 63) >> 3, grid_row & 7
    flip = 7 * (grid_lane >> 6)
    for t in range(8):
        a, b = (second, first) if t % 4 >= 2 else (first, second)
        b = b ^ 7 if t % 2 == 1 else b
        source = 8 * (a ^ flip) + b
        fits = (source == (grid_lane & 63)) & ((grid_row < 64) if t < 4 else (grid_row >= 64))
        perm[:, pl.ds(t * LANES, LANES)] = fits.astype(F32).astype(BF16)

    @pl.when(core == 1)
    def _():
        pl.semaphore_wait(barrier, 2 * (n_z - 1))
        pl.semaphore_signal(ready, inc=1, **at_device(2 * z, y))

    await_all(0, rc1, n_p)
    mine = jnp.sum(rc1[...], axis=0)
    own2[...] = mine
    rc2[z] = mine

    @pl.when(core == 0)
    def _():
        pl.semaphore_wait(ready, 1)

    send_line(own2, rc2, 1)

    def sum_of(coef, slabs, a):
        total = coef(0, a) * slabs(0)
        for m in range(1, EDGE):
            total = total + coef(m, a) * slabs(m)
        return total

    def per_row(body):
        def step(a, c):
            body(a)
            return c

        lax.fori_loop(0, EDGE, step, 0)

    def slab_i(ref):
        return lambda m: ref[pl.ds(pl.multiple_of(64 * m, 64), 64), :]

    def slab_j(ref):
        cube = ref.reshape(EDGE, EDGE, EDGE, LANES)
        return lambda m: cube[:, m].reshape(64, LANES)

    def forward(d):
        return lambda m, a: fdm[d, m, pl.ds(a, 1), :]

    def backward(d):
        return lambda m, a: fdm[d, a, m : m + 1, :]

    def put_i(ref, a, value):
        ref[pl.ds(pl.multiple_of(64 * a, 64), 64), :] = value

    def put_j(ref, a, value):
        ref.reshape(EDGE, EDGE, EDGE, LANES)[:, pl.ds(a, 1)] = value.reshape(EDGE, 1, EDGE, LANES)

    loads["fdm"].wait()
    loads["eig"].wait()
    per_row(lambda a: put_i(buf_a, a, sum_of(forward(0), slab_i(rm), a)))
    per_row(lambda a: put_j(buf_b, a, sum_of(forward(1), slab_j(buf_a), a)))
    for k in range(EDGE):
        turned[pl.ds(64 * k, 64), :] = buf_b[pl.ds(k, 64, stride=EDGE), :]
    base = jnp.concatenate([eig_ref[0, a : a + 1, :] + eig_ref[1] for a in range(EDGE)], axis=0)
    buf_a[pl.ds(0, 64), :] = base

    def spectral(a):
        value = sum_of(forward(2), slab_i(turned), a)
        put_i(buf_b, a, value / (buf_a[pl.ds(0, 64), :] + eig_ref[2, pl.ds(a, 1), :]))

    per_row(spectral)

    per_row(lambda a: put_i(turned, a, sum_of(backward(2), slab_i(buf_b), a)))
    for k in range(EDGE):
        buf_a[pl.ds(k, 64, stride=EDGE), :] = turned[pl.ds(64 * k, 64), :]
    per_row(lambda a: put_j(buf_b, a, sum_of(backward(1), slab_j(buf_a), a)))
    per_row(lambda a: put_i(field, a, sum_of(backward(0), slab_i(buf_b), a)))

    def face_of(ref, f):
        if f < 2:
            return ref[pl.ds(448 * f, 64), :]
        if f < 4:
            return slab_j(ref)(7 * (f - 2))
        return ref[pl.ds(7 * (f - 4), 64, stride=EDGE), :]

    def send_faces(ref, out, inc, phase):
        for f in range(6):
            high, low = split(face_of(ref, f))
            faces[0:64, pl.ds(f * LANES, LANES)] = high
            faces[64:128, pl.ds(f * LANES, LANES)] = low
        found = lax.dot_general(onehot[...], faces[...], NT, preferred_element_type=F32)
        found = found + pltpu.roll(found, 64, 1)
        out[...] = found
        inc[pl.ds(FIRST, 32), :] = found[0:32]
        hops = [
            (PEER_ROW + PEER_ROWS * g, PEER_ROW + PEER_ROWS * back_to[g], PEER_ROWS, (x, lax.rem(y + offsets[g], n_y)))
            for g in range(5)
        ] + [
            (
                PIPE_ROW + PIPE_ROWS * s,
                PIPE_ROW + PIPE_ROWS * (1 - s),
                PIPE_ROWS,
                (lax.rem(x + n_x - 1 + 2 * s, n_x), y),
            )
            for s in range(2)
        ]
        for start, land, count, target in hops:
            send(out.at[pl.ds(start, count)], inc.at[pl.ds(land, count)], phase, *target)
        sent.append((phase, inc.at[pl.ds(0, SENT_ROWS)]))

    def await_faces(phase, inc):
        some = inc.at[pl.ds(0, SENT_ROWS)]
        pltpu.make_async_copy(some, some, recv_sem.at[phase]).wait()

    def place_faces(ref, inc):
        high, low = split(inc[pl.ds(FIRST, USED), :])
        for p in range(4):
            mask = masks[:, pl.ds(p * LANES, LANES)]
            picked[:, pl.ds(p * LANES, LANES)] = high * mask
            picked[:, pl.ds((p + 4) * LANES, LANES)] = low * mask
        across = lax.dot_general(perm[...], picked[...], NT, preferred_element_type=F32)
        extra = jnp.dot(across.astype(BF16), onehot[pl.ds(FIRST, USED), :], preferred_element_type=F32)
        extra = extra[0:64] + extra[64:128]
        cube = ref.reshape(EDGE, EDGE, EDGE, LANES)
        for f in range(6):
            more = extra[:, f * LANES : (f + 1) * LANES]
            if f < 2:
                ref[pl.ds(448 * f, 64), :] += more
            elif f < 4:
                cube[:, 7 * (f - 2)] += more.reshape(EDGE, EDGE, LANES)
            else:
                at = pl.ds(7 * (f - 4), 64, stride=EDGE)
                ref[at, :] = ref[at, :] + more

    await_all(9, block, n_p)
    keep.wait()
    for n in range(n_p):
        high, low = split(block[n])
        blocks[16 * n : 16 * n + 16, :] = high
        blocks[16 * (n_p + n) : 16 * (n_p + n) + 16, :] = low

    await_all(1, rc2, n_z)
    mine = jnp.sum(rc2[...], axis=0)
    high, low = split(jnp.concatenate([mine[0:1], mine[1:2]], axis=1))
    pair = jnp.concatenate([high.astype(F32), low.astype(F32), jnp.zeros((14, 2 * LANES), F32)], axis=0).astype(BF16)
    product = lax.dot_general(pair, blocks[...], NT, preferred_element_type=F32)
    count = 16 * n_p
    product = product[0:1, :count] + (product[1:2, :count] + product[0:1, count:])
    mine = jnp.concatenate([product[:, LANES * h : LANES * h + LANES] for h in range(4)], axis=0)
    own3[...] = mine
    rc3[me] = mine
    send_plane(lambda t: own3, rc3, 2)

    send_faces(field, out1, inc1, 7)

    await_all(2, rc3, n_p)
    mine = jnp.sum(rc3[...], axis=0)
    own4[...] = mine
    rc4[z] = mine
    send_line(own4, rc4, 3)
    await_faces(7, inc1)
    place_faces(field, inc1)
    loads["diag"].wait()
    loads["cross"].wait()

    await_all(3, rc4, n_z)
    for q in range(n_z):
        coarse[pl.ds(4 * q, 4), :] = rc4[q]

    high, low = split(coarse[...])
    at_low = jnp.dot(jnp.concatenate([high, low], axis=0), y_one[...], preferred_element_type=F32)
    corner = jnp.sum((at_low[0:64] + at_low[64:128]) * h_one[...], axis=0, keepdims=True)
    planes = []
    for ci in range(2):
        lines = []
        for cj in range(2):
            at = (4 * ci + 2 * cj) * LANES
            lines.append(hat_rows[0] * corner[:, at : at + LANES] + hat_rows[1] * corner[:, at + LANES : at + 2 * LANES])
        planes.append(
            jnp.concatenate(
                [float(HATS[0, j]) * lines[0] + float(HATS[1, j]) * lines[1] for j in range(EDGE)], axis=0
            )
        )
    for i in range(EDGE):
        at = pl.ds(64 * i, 64)
        lifted = float(HATS[0, i]) * planes[0] + float(HATS[1, i]) * planes[1]
        direction[at, :] = alive * (field[at, :] + lifted)

    def take(ref, start, stride):
        return [ref[pl.ds(pl.multiple_of(start + stride * m, 8), 8), :] for m in range(EDGE)]

    def along_first(j, c):
        result = mirrored(D_EVEN, D_ODD, take(direction, 8 * j, 64))
        for a in range(EDGE):
            grad1[pl.ds(pl.multiple_of(64 * a + 8 * j, 8), 8), :] = result[a]
        return c

    lax.fori_loop(0, EDGE, along_first, 0)

    def turn(values, ref):
        for m in range(EDGE):
            ref[pl.ds(EDGE * m, EDGE), :] = values[m]
        return [ref[pl.ds(m, EDGE, stride=EDGE), :] for m in range(EDGE)]

    def middle(i, sums):
        curve, dots = sums
        start = pl.multiple_of(64 * i, 64)
        slab = pl.ds(start, 64)
        d = take(direction, start, 8)
        across = turn(d, turned.at[pl.ds(0, 64)])
        g3 = turn(mirrored(D_EVEN, D_ODD, across), turned.at[pl.ds(64, 64)])
        g2 = mirrored(D_EVEN, D_ODD, d)
        g1 = take(grad1, start, 8)
        m = [diag[q, slab, :].astype(F32) for q in range(3)] + [cross[q, slab, :].astype(F32) for q in range(3)]
        f2, f3 = [], []
        for j in range(EDGE):
            rr, ss, tt, rs, rt, st = [q[8 * j : 8 * j + 8] for q in m]
            u = rr * g1[j] + rs * g2[j] + rt * g3[j]
            v = rs * g1[j] + ss * g2[j] + st * g3[j]
            w = rt * g1[j] + st * g2[j] + tt * g3[j]
            curve = curve + (g1[j] * u + g2[j] * v) + (g3[j] * w + d[j] * d[j])
            grad1[pl.ds(start + 8 * j, 8), :] = u
            f2.append(v)
            f3.append(w)
        dots = dots + jnp.sum((rm[slab, :] * direction[slab, :]).reshape(EDGE, EDGE, LANES), axis=0)
        b3 = turn(mirrored(T_EVEN, T_ODD, turn(f3, turned2.at[pl.ds(0, 64)])), turned2.at[pl.ds(64, 64)])
        b2 = mirrored(T_EVEN, T_ODD, f2)
        for j in range(EDGE):
            field[pl.ds(start + 8 * j, 8), :] = (b2[j] + b3[j]) + d[j]
        return curve, dots

    zero = jnp.zeros((EDGE, LANES), F32)
    curve, dots = lax.fori_loop(0, EDGE, middle, (zero, zero))

    def back_first(j, c):
        result = mirrored(T_EVEN, T_ODD, take(grad1, 8 * j, 64))
        for a in range(EDGE):
            at = pl.ds(pl.multiple_of(64 * a + 8 * j, 8), 8)
            field[at, :] = field[at, :] + result[a]
        return c

    lax.fori_loop(0, EDGE, back_first, 0)

    send_faces(field, out2, inc2, 8)

    def folded(a, b):
        return jnp.sum((a * b).reshape(POINTS // EDGE, EDGE, LANES), axis=0)

    old = folded(rm[...], rm[...])
    loads["sol"].wait()
    sol[...] = sol[...] * alive
    await_faces(8, inc2)
    place_faces(field, inc2)

    image = field[...]
    mixed = folded(rm[...], image)
    square = folded(image, image)
    sums = jnp.zeros((1, LANES), F32)
    for q, value in enumerate((dots, curve, old, mixed, square)):
        one = jnp.sum(jnp.sum(value, axis=0, keepdims=True), axis=1, keepdims=True)
        sums = jnp.where(lane == q, one, sums)
    own_a[...] = sums
    rc_a[me] = sums
    send_plane(lambda t: own_a, rc_a, 5)
    await_all(5, rc_a, n_p)
    sums = jnp.sum(rc_a[...], axis=0)
    own_b[...] = sums
    rc_b[z] = sums
    send_line(own_b, rc_b, 6)
    await_all(6, rc_b, n_z)
    sums = jnp.sum(rc_b[...], axis=0)

    totals[...] = sums
    for phase, some in sent:
        pltpu.make_async_copy(some, some, send_sem.at[phase]).wait()


def update(sol, res, direction, image, sums_ref, sol_out, res_out, ratio_out, moved, left, sem):
    lane = iota((1, LANES), 1)
    sums = sums_ref[...]

    def total(q):
        return jnp.sum(jnp.where(lane == q, sums, 0.0), axis=1, keepdims=True)

    step = total(0) / total(1)
    parts = 4
    rows = POINTS // parts
    stores = []
    for h in range(parts):
        at = pl.ds(rows * h, rows)
        for q, (ref, value, out) in enumerate(
            ((moved, sol[at, :] + step * direction[at, :], sol_out), (left, res[at, :] - step * image[at, :], res_out))
        ):
            ref[at, :] = value
            store = pltpu.make_async_copy(ref.at[at], out.at[at], sem.at[h, q])
            store.start()
            stores.append(store)
    ratio = (total(2) - 2.0 * step * total(3) + step * step * total(4)) / total(2)
    ratio_out[0] = jnp.sum(ratio)
    for store in stores:
        store.wait()


def on_device(n_x, n_y, *args):
    live, vid, eig, sface, scode, pface, pcode = (args[i] for i in (8, 6, 5, 9, 10, 11, 12))
    smem = pl.BlockSpec(memory_space=pltpu.SMEM)
    vmem = pl.BlockSpec(memory_space=pltpu.VMEM)
    hbm = pl.BlockSpec(memory_space=pl.ANY)
    n_p, n_z = 2 * n_y, n_x // 2
    field = pltpu.VMEM((POINTS, LANES), F32)
    whole = jax.ShapeDtypeStruct((POINTS, LANES), F32)
    held = [field] * 4 + [pltpu.VMEM((1, LANES), F32)]
    results = pl.pallas_call(
        functools.partial(kernel, n_x, n_y),
        out_shape=held,
        in_specs=[hbm] * 13,
        out_specs=[vmem] * 5,
        scratch_shapes=[
            pltpu.SMEM((1,), jnp.int32),
            pltpu.VMEM(vid.shape, jnp.int32),
            pltpu.VMEM(eig.shape, F32),
            pltpu.VMEM(sface.shape, jnp.int32),
            pltpu.VMEM(scode.shape, jnp.int32),
            pltpu.VMEM(pface.shape, jnp.int32),
            pltpu.VMEM(pcode.shape, jnp.int32),
            pltpu.VMEM((3, POINTS, LANES), BF16),
            pltpu.VMEM((3, POINTS, LANES), BF16),
            pltpu.VMEM((3, EDGE, EDGE, LANES), F32),
            pltpu.VMEM((n_p, 16, 2 * LANES), F32),
            pltpu.VMEM((32 * n_p, 2 * LANES), BF16),
            field,
            field,
            field,
            field,
            field,
            pltpu.VMEM((LANES, 8 * LANES), BF16),
            pltpu.VMEM((LANES, 8 * LANES), BF16),
            pltpu.VMEM((64, 8 * LANES), F32),
            pltpu.VMEM((n_p, 2, LANES), F32),
            pltpu.VMEM((n_p, 2, LANES), F32),
            pltpu.VMEM((2, LANES), F32),
            pltpu.VMEM((n_z, 2, LANES), F32),
            pltpu.VMEM((4, LANES), F32),
            pltpu.VMEM((n_p, 4, LANES), F32),
            pltpu.VMEM((4, LANES), F32),
            pltpu.VMEM((n_z, 4, LANES), F32),
            pltpu.VMEM((64, LANES), F32),
            pltpu.VMEM((ROWS, LANES), F32),
            pltpu.VMEM((USED, LANES), F32),
            pltpu.VMEM((ROWS, 6 * LANES), BF16),
            pltpu.VMEM((USED, 4 * LANES), BF16),
            pltpu.VMEM((LANES, 8 * LANES), BF16),
            pltpu.VMEM((LANES, 6 * LANES), BF16),
            pltpu.VMEM((ROWS, LANES), F32),
            pltpu.VMEM((ROWS, LANES), F32),
            pltpu.VMEM((ROWS, LANES), F32),
            pltpu.VMEM((ROWS, LANES), F32),
            pltpu.VMEM((USED, 8 * LANES), BF16),
            pltpu.VMEM((1, LANES), F32),
            pltpu.VMEM((n_p, 1, LANES), F32),
            pltpu.VMEM((1, LANES), F32),
            pltpu.VMEM((n_z, 1, LANES), F32),
            pltpu.SemaphoreType.REGULAR,
            pltpu.SemaphoreType.DMA((14,)),
            pltpu.SemaphoreType.DMA((10,)),
            pltpu.SemaphoreType.DMA((10,)),
        ],
        compiler_params=pltpu.CompilerParams(
            collective_id=0, has_side_effects=True, vmem_limit_bytes=60 * 1024 * 1024
        ),
    )(*args)
    return pl.pallas_call(
        update,
        out_shape=(whole, whole, jax.ShapeDtypeStruct((1,), F32)),
        in_specs=[vmem] * 5,
        out_specs=(hbm, hbm, smem),
        scratch_shapes=[field, field, pltpu.SemaphoreType.DMA((4, 2))],
        compiler_params=pltpu.CompilerParams(vmem_limit_bytes=60 * 1024 * 1024),
    )(*[pltpu.with_memory_space_constraint(r, pltpu.VMEM) for r in results])


def solution(mesh):
    both = ("gx", "gy")
    placed = (
        P(None, both),
        P(None, both),
        P(None, None, both),
        P(None, None, both),
        P(None, None, None, both),
        P(None, None, both),
        P(None, both),
        P(both, None),
        P(both),
        P(both, None, None),
        P(both, None, None),
        P(both, None, None),
        P(both, None, None),
    )
    return jax.shard_map(
        functools.partial(on_device, mesh.shape["gx"], mesh.shape["gy"]),
        mesh=mesh,
        in_specs=placed,
        out_specs=(P(None, both), P(None, both), P()),
        check_vma=False,
    )
```
